256 devices in a mesh: dp: 2 (over core), expert: 128 (over y, z, x).
Axes of the slice: x: 4, y: 4, z: 8, core: 2. Of those that a mesh axis runs over, the one named last changes fastest.
Arguments:
- tokens: bfloat16 [32768, 1536], P(('dp', 'expert')), may hold values from -6 to 6
- out_grad: bfloat16 [32768, 1536], P(('dp', 'expert')), may hold values from -1.1953125 to 1.1953125
- routes: int32 [32768, 2], P(('dp', 'expert')), may hold values from 0 to 63, all different within a row; in each aligned block of 128 rows (0 to 127, 128 to 255, ...) at most 5 rows name the same one
- gate_probs: float32 [32768, 2], P(('dp', 'expert')), may hold values from 0.2 to 1
- weight_in: bfloat16 [1536, 196608], P('dp', 'expert'), may hold values from -0.15625 to 0.15625
- weight_out: bfloat16 [196608, 1536], P('expert', 'dp'), may hold values from -0.109375 to 0.109375
Outputs:
- token_grad: bfloat16 [32768, 1536], P(('dp', 'expert'))
- grad_in: bfloat16 [1536, 196608], P('dp', 'expert')
- grad_out: bfloat16 [196608, 1536], P('expert', 'dp')
The draws below stay inside these ranges and needn't reach their ends.
Inputs may be any that keep to these rules, and one draw needn't show every extreme that they name: `routes`: within the rows of one device, no expert is named by more than 5 slots, and in every draw some expert is named by exactly 5 slots on some device; a token names two different experts; every expert is named somewhere.
All inputs are finite; a program needn't handle non-finite values.
Results may differ from the reference program's by a relative error of at most 0.012.
Values may be sent and summed in bfloat16 or wider, within the bound.
No kernel may reach another device: no remote copies, remote signals or barrier semaphores. Data moves between devices by JAX's collectives and lax.ppermute only.
A program may use at most 128 MiB of HBM per device.

```python
import math
import jax
import jax.numpy as jnp
import numpy as np
from jax import lax

D = 1536
HID = 3072
TOK_DEV = 128
EXPERTS = 64
HID_DEV = 1536
CAP = 5
TOKENS = 32768
DEVICES = 256


def block_levels(own_key, dims, pieces, least, high):
    level = 1.0
    for dim, shards_of in pieces:
        steps = jax.random.uniform(jax.random.fold_in(jax.random.fold_in(own_key, 6), dim), (shards_of,), jnp.float32, least / len(pieces), high / len(pieces))
        level = level * jnp.repeat(jnp.exp(steps), dims[dim] // shards_of).reshape((-1,) + (1,) * (len(dims) - 1 - dim))
    return level


def shared_out(own_key, own, number, rows, number_of, top, bound, lean):
    ranking = jax.random.permutation(own_key, number_of)
    heavy_load, common = portions_of(number_of, rows * top, bound, lean, True), portions_of(number_of, rows * top, bound, lean, False)
    places = jnp.arange(number_of)

    def named(lengths, offset_by):
        used = int((lengths > 0).sum())
        fixed = max(1, used // 4)
        passed = fixed + (places - fixed + offset_by * (used - fixed)) % max(1, number_of - fixed)
        return jnp.zeros((number_of,), jnp.int32).at[ranking[jnp.where(places < fixed, places, passed)]].set(jnp.asarray(lengths, jnp.int32))

    lengths = jnp.where(number % 4 == 0, named(heavy_load, number // 4), named(common, number - number // 4 - 1))
    mixed = jax.random.permutation(jax.random.fold_in(own, 3), number_of)
    source_of, sink = mixed[0:number_of // 2 * 2:2], mixed[1:number_of // 2 * 2:2]
    margin = jnp.minimum(lengths[source_of] - 1, bound - lengths[sink]) // 2
    margin = jnp.where((source_of == ranking[0]) | (sink == ranking[0]) | (lengths[sink] == 0), 0, jnp.maximum(margin, 0))
    passed = jax.random.randint(jax.random.fold_in(own, 4), (number_of // 2,), 0, 1 << 20) % (margin + 1)
    lengths = lengths.at[source_of].add(-passed).at[sink].add(passed)
    items = jnp.searchsorted(jnp.cumsum(lengths), jnp.arange(rows * top), side="right").astype(jnp.int32)
    listing = items.reshape(top, rows).T
    listing = listing[jax.random.permutation(jax.random.fold_in(own, 1), rows)]
    offset_by = jax.random.randint(jax.random.fold_in(own, 2), (rows, 1), 0, top)
    return jnp.take_along_axis(listing, (jnp.arange(top)[None, :] + offset_by) % top, axis=1)


def portions_of(amount, total, most, slope, full):
    weights = [(1 << 20) // math.isqrt(standing ** slope) + 1 for standing in range(1, amount + 1)]
    largest = most if full else min(most, max(-(-total // amount), total * weights[0] // sum(weights)))
    least = 1 if total - largest >= amount - 1 else 0
    counts, rest = [largest] + [least] * (amount - 1), total - largest - least * (amount - 1)
    while rest > 0:
        free = [i for i in range(1, amount) if counts[i] < largest] or [i for i in range(1, amount) if counts[i] < most]
        mass, remaining = sum([weights[i] for i in free]), rest
        for i in free:
            more = min(most - counts[i], max(1, remaining * weights[i] // mass), rest)
            counts[i] = counts[i] + more
            rest = rest - more
    return np.array(counts)


def gaussian(stream_key, shape, scale, limit, shards=(), held_as=jnp.bfloat16):
    array = scale * jax.random.normal(stream_key, shape, jnp.float32)
    if shards:
        array = array * block_levels(stream_key, shape, shards, -0.22, 0.18)
    return jnp.clip(array, -limit, limit).astype(held_as)


def setup_inputs(seed: int = 0) -> dict:
    key_of = jax.random.split(jax.random.key(seed), 7)
    tokens = gaussian(key_of[0], (TOKENS, D), 1.0, 6.0, ((0, 256),))
    out_grad = gaussian(key_of[1], (TOKENS, D), 0.2, 1.1953125, ((0, 256),))
    routes_keys = jax.random.split(jax.random.fold_in(key_of[2], 1), TOKENS // TOK_DEV)
    routes_turns = jax.random.permutation(jax.random.fold_in(key_of[2], 3), TOKENS // TOK_DEV)
    routes = jax.vmap(lambda own, number: shared_out(jax.random.fold_in(key_of[2], 2), own, number, TOK_DEV, EXPERTS, 2, CAP, 2))(routes_keys, routes_turns).reshape((TOKENS, 2))
    gate_probs = jnp.clip(0.2 + 0.8 * jax.random.uniform(key_of[3], (TOKENS, 2), jnp.float32) ** block_levels(key_of[3], (TOKENS, 2), ((0, 256),), -0.2, 0.2), 0.2, 1.0)
    weight_in = gaussian(key_of[4], (D, EXPERTS * HID), D ** -0.5, 0.15625, ((0, 2), (1, 128)))
    weight_out = gaussian(key_of[5], (EXPERTS * HID, D), HID ** -0.5, 0.109375, ((0, 128), (1, 2)))
    return {"tokens": tokens, "out_grad": out_grad, "routes": routes, "gate_probs": gate_probs, "weight_in": weight_in, "weight_out": weight_out}


root_two_pi = 0.7978845608
cubic_term = 0.044715


def gelu_value(pre):
    inner = root_two_pi * (pre + cubic_term * pre * pre * pre)
    return 0.5 * pre * (1.0 + jnp.tanh(inner))


def gelu_slope(pre):
    inner = root_two_pi * (pre + cubic_term * pre * pre * pre)
    tanh_value = jnp.tanh(inner)
    return 0.5 * (1.0 + tanh_value) + 0.5 * pre * (1.0 - tanh_value * tanh_value) * root_two_pi * (1.0 + 3.0 * cubic_term * pre * pre)


def slot_targets(route_block, expert_count, capacity):
    slot_expert = route_block.reshape(-1)
    labels = jnp.arange(expert_count, dtype=jnp.int32)
    one_hot = (slot_expert[:, None] == labels[None, :]).astype(jnp.int32)
    before = jnp.cumsum(one_hot, axis=0) - one_hot
    return slot_expert * capacity + jnp.sum(before * one_hot, axis=1)


def pack_rows(tokens, out_grad, routes, gate_probs, expert_count, capacity):
    target = slot_targets(routes, expert_count, capacity)
    slot_count = target.shape[0]
    places = jnp.arange(expert_count * capacity, dtype=jnp.int32)
    match = (target[None, :] == places[:, None]).astype(jnp.int32)
    source_slot = jnp.sum(match * jnp.arange(slot_count, dtype=jnp.int32)[None, :], axis=1)
    filled = jnp.sum(match, axis=1).astype(jnp.float32)[:, None]
    token_index = source_slot // 2
    token_rows = (tokens[token_index].astype(jnp.float32) * filled).astype(jnp.bfloat16)
    scale = gate_probs.reshape(-1)[source_slot][:, None] * filled
    grad_rows = (out_grad[token_index].astype(jnp.float32) * scale).astype(jnp.bfloat16)
    return target, token_rows, grad_rows


def expert_half(token_rows, grad_rows, w_first, w_second):
    pre = jnp.dot(token_rows, w_first, preferred_element_type=jnp.float32)
    hidden = gelu_value(pre).astype(jnp.bfloat16)
    back = lax.dot_general(grad_rows, w_second, (((1,), (1,)), ((), ())), preferred_element_type=jnp.float32)
    d_pre = (back * gelu_slope(pre)).astype(jnp.bfloat16)
    part = lax.dot_general(d_pre, w_first, (((1,), (1,)), ((), ())), preferred_element_type=jnp.float32).astype(jnp.bfloat16)
    return hidden, d_pre, part


def contract_rows(left, right):
    return lax.dot_general(left, right, (((0,), (0,)), ((), ())), preferred_element_type=jnp.float32)


def reference(tokens, out_grad, routes, gate_probs, weight_in, weight_out):
    def pack_block(token_block, grad_block, route_block, gate_block):
        return pack_rows(token_block, grad_block, route_block, gate_block, EXPERTS, CAP)

    target, token_rows, grad_rows = jax.vmap(pack_block)(
        tokens.reshape(DEVICES, TOK_DEV, D), out_grad.reshape(DEVICES, TOK_DEV, D),
        routes.reshape(DEVICES, TOK_DEV, 2), gate_probs.reshape(DEVICES, TOK_DEV, 2))

    def by_expert(packed):
        return packed.reshape(DEVICES, EXPERTS, CAP, D).transpose(1, 0, 2, 3).reshape(EXPERTS, DEVICES * CAP, D)

    def one_expert(inputs):
        expert_id, token_part, grad_part = inputs
        w_first = lax.dynamic_slice_in_dim(weight_in, expert_id * HID, HID, 1)
        w_second = lax.dynamic_slice_in_dim(weight_out, expert_id * HID, HID, 0)
        parts = []
        first_grads = []
        second_grads = []
        for half_index in range(2):
            first_half = w_first[:, half_index * HID_DEV:(half_index + 1) * HID_DEV]
            second_half = w_second[half_index * HID_DEV:(half_index + 1) * HID_DEV, :]
            hidden, d_pre, part = expert_half(token_part, grad_part, first_half, second_half)
            parts.append(part)
            first_grads.append(contract_rows(token_part, d_pre))
            second_grads.append(contract_rows(hidden, grad_part))
        slot_grad = (parts[0].astype(jnp.float32) + parts[1].astype(jnp.float32)).astype(jnp.bfloat16)
        first_grad = jnp.concatenate(first_grads, axis=1).astype(jnp.bfloat16)
        second_grad = jnp.concatenate(second_grads, axis=0).astype(jnp.bfloat16)
        return slot_grad, first_grad, second_grad

    slot_grads, first_parts, second_parts = lax.map(
        one_expert, (jnp.arange(EXPERTS, dtype=jnp.int32), by_expert(token_rows), by_expert(grad_rows)))
    grad_in = first_parts.transpose(1, 0, 2).reshape(D, EXPERTS * HID)
    grad_out = second_parts.reshape(EXPERTS * HID, D)
    returned = slot_grads.reshape(EXPERTS, DEVICES, CAP, D).transpose(1, 0, 2, 3).reshape(DEVICES, EXPERTS * CAP, D)

    def pick_rows(block_rows, place_index):
        return block_rows[place_index]

    picked = jax.vmap(pick_rows)(returned, target)
    token_grad = picked.reshape(TOKENS, 2, D).astype(jnp.float32).sum(axis=1).astype(jnp.bfloat16)
    return token_grad, grad_in, grad_out
```

```python
import functools

import jax
import jax.numpy as jnp
from jax import lax
from jax.experimental import pallas as pl
from jax.experimental.pallas import tpu as pltpu
from jax.sharding import PartitionSpec as P

ROOT_TWO_PI = 0.7978845608
CUBIC = 0.044715
BF = jnp.bfloat16
F32 = jnp.float32
D = 1536
TOK = 128
EXPERTS = 64
BLOCK = 768


def iota(shape, dim):
    return lax.broadcasted_iota(jnp.int32, shape, dim)


def mask(condition):
    return jnp.where(condition, 1.0, 0.0).astype(BF)


def dot(a, b):
    return jnp.dot(a, b, preferred_element_type=F32)


def dot_nt(a, b):
    return lax.dot_general(a, b, (((1,), (1,)), ((), ())), preferred_element_type=F32)


def dot_tn(a, b):
    return lax.dot_general(a, b, (((0,), (0,)), ((), ())), preferred_element_type=F32)


def whole(shape):
    return pl.BlockSpec(shape, lambda *_: (0,) * len(shape))


def params(mib=40):
    return pltpu.CompilerParams(vmem_limit_bytes=mib * 2**20)


def slot_matches(routes_t):
    expert = iota((EXPERTS * 8, TOK), 0) >> 3
    first = routes_t[0:1, :] == expert
    match = first | (routes_t[1:2, :] == expert)
    earlier = mask(iota((TOK, TOK), 0) < iota((TOK, TOK), 1))
    rank = dot(mask(match), earlier)
    return first, match, rank


def pack_kernel(routes_ref, gates_ref, tokens_ref, grads_ref, main_ref, last_ref):
    first, match, rank = slot_matches(routes_ref[...])
    gate = jnp.where(first, gates_ref[0:1, :], gates_ref[1:2, :])
    inner = iota((EXPERTS * 8, TOK), 0) & 7

    def scale_of(chosen):
        return jnp.sum(jnp.where(chosen, gate, 0.0), axis=1, keepdims=True)

    place = jnp.where(inner < 3, inner, inner - 3)
    chosen = match & (rank == place.astype(F32)) & (inner < 6)
    from_tokens, from_grads, scale = mask(chosen & (inner < 3)), mask(chosen & (inner >= 3)), scale_of(chosen)
    for j in range(3):
        columns = slice(j * 384, (j + 1) * 384)
        rows = dot(from_tokens, tokens_ref[:, columns])
        rows += dot(from_grads, grads_ref[:, columns]) * scale
        chosen = match & (rank == float(j))
        rows += dot(mask(chosen & (inner == 6)), tokens_ref[:, 1152:])
        rows += dot(mask(chosen & (inner == 7)), grads_ref[:, 1152:]) * scale_of(chosen)
        main_ref[:, columns] = rows.astype(BF)

    quarter = inner & 3
    chosen = match & (rank == (3 + (quarter & 1)).astype(F32))
    scale = scale_of(chosen)
    rows = jnp.zeros((EXPERTS * 8, 768), F32)
    for j in range(2):
        side = chosen & ((inner >> 2) == j)
        columns = slice(j * 768, (j + 1) * 768)
        rows += dot(mask(side & (quarter < 2)), tokens_ref[:, columns])
        rows += dot(mask(side & (quarter >= 2)), grads_ref[:, columns]) * scale
    last = rows.astype(BF)
    last_ref[0:512, :] = last
    last_ref[512:1024, :] = last


def pack(routes_t, gates_t, tokens, out_grad):
    return pl.pallas_call(
        pack_kernel,
        out_shape=(
            jax.ShapeDtypeStruct((512, 1152), BF),
            jax.ShapeDtypeStruct((1024, 768), BF),
        ),
        compiler_params=params(),
        cost_estimate=pl.CostEstimate(flops=10**9, bytes_accessed=5 * 10**6, transcendentals=0),
        name="pack",
    )(routes_t, gates_t, tokens, out_grad)


def unpack(last, got_ref, token_ref, grad_ref):
    row, column = iota((256, 256), 0), iota((256, 256), 1)
    move = mask(column == ((row & 31) << 3) + (row >> 5))
    for g in range(got_ref.shape[0] // 256):
        rows = dot(move, got_ref[g * 256:(g + 1) * 256, :]).astype(BF)
        if last:
            for j in range(2):
                columns = slice(j * 768, (j + 1) * 768)
                token_ref[g * 64:(g + 1) * 64, columns] = rows[j * 128:j * 128 + 64]
                grad_ref[g * 64:(g + 1) * 64, columns] = rows[j * 128 + 64:j * 128 + 128]
        else:
            token_ref[g * 96:(g + 1) * 96, :1152] = rows[:96]
            grad_ref[g * 96:(g + 1) * 96, :1152] = rows[96:192]
            for j in range(3):
                target = slice(g * 96 + j * 32, g * 96 + (j + 1) * 32)
                token_ref[target, 1152:] = rows[192:224, j * 384:(j + 1) * 384]
                grad_ref[target, 1152:] = rows[224:256, j * 384:(j + 1) * 384]


def expert_kernel(last, group_ref, got_ref, w1_ref, w2_ref, token_ref, grad_ref, hidden_ref, dpre_ref, *rest):
    *part_refs, total = rest
    step = pl.program_id(0)

    @pl.when(step == 0)
    def _():
        unpack(last, got_ref, token_ref, grad_ref)

    pre = dot(token_ref[...], w1_ref[...])
    back = dot_nt(grad_ref[...], w2_ref[...])
    square = pre * pre
    th = jnp.tanh(ROOT_TWO_PI * (pre + CUBIC * square * pre))
    half = 0.5 * (1.0 + th)
    hidden_ref[...] = (pre * half).astype(BF)
    slope = half + 0.5 * pre * (1.0 - th * th) * ROOT_TWO_PI * (1.0 + 3.0 * CUBIC * square)
    d_pre = (back * slope).astype(BF)
    dpre_ref[...] = d_pre
    term = dot_nt(d_pre, w1_ref[...])

    @pl.when(step == 0)
    def _():
        total[...] = term

    @pl.when(step > 0)
    def _():
        total[...] += term

    @pl.when(step == pl.num_programs(0) - 1)
    def _():
        if last:
            for k, part_ref in enumerate(part_refs):
                group = group_ref[0] if k == 0 else 1 - group_ref[0]
                part_ref[...] = total[pl.ds(pl.multiple_of(group * 128, 128), 128), :].astype(BF)
        else:
            part_refs[0][...] = total[...].astype(BF)


def expert_rows(last, group, got, w1, w2):
    rows = 256 if last else 192
    parts = [(128, D)] * 2 if last else [(192, D)]
    hidden_units = w1.shape[1]
    row_shape = jax.ShapeDtypeStruct((rows, D), BF)
    hid_shape = jax.ShapeDtypeStruct((rows, hidden_units), BF)
    return pl.pallas_call(
        functools.partial(expert_kernel, last),
        grid=(hidden_units // BLOCK,),
        in_specs=[
            pl.BlockSpec(memory_space=pltpu.SMEM),
            whole(got.shape),
            pl.BlockSpec((D, BLOCK), lambda h: (0, h)),
            pl.BlockSpec((BLOCK, D), lambda h: (h, 0)),
        ],
        out_specs=(
            whole((rows, D)),
            whole((rows, D)),
            pl.BlockSpec((rows, BLOCK), lambda h: (0, h)),
            pl.BlockSpec((rows, BLOCK), lambda h: (0, h)),
            *(whole(part) for part in parts),
        ),
        out_shape=(
            row_shape, row_shape, hid_shape, hid_shape, *(jax.ShapeDtypeStruct(part, BF) for part in parts)
        ),
        scratch_shapes=[pltpu.VMEM((rows, D), F32)],
        compiler_params=params(32),
        cost_estimate=pl.CostEstimate(
            flops=6 * rows * D * hidden_units, bytes_accessed=14 * 10**6, transcendentals=rows * hidden_units
        ),
        name="expert_last" if last else "expert_main",
    )(group, got, w1, w2)


def merge_kernel(main_a, main_b, last_a, last_b, out_ref):
    row, column = iota((256, 128), 0), iota((256, 128), 1)
    target = ((column & 31) << 3) + (column >> 5)
    row6, column6 = iota((256, 192), 0), iota((256, 192), 1)
    spread = mask(row6 == ((column6 & 31) << 3) + (column6 >> 5))
    for g in range(2):
        a, b = slice(g * 96, (g + 1) * 96), slice(g * 64, (g + 1) * 64)
        three = (main_a[a, :].astype(F32) + main_b[a, :].astype(F32)).astype(BF)
        two = (last_a[b, :].astype(F32) + last_b[b, :].astype(F32)).astype(BF)
        four = jnp.concatenate([three, two[:32]], axis=0)
        folded = dot(mask(row == target), four[:, :768]) + dot(mask(row == target + 4), four[:, 768:])
        out_ref[g * 256:(g + 1) * 256, :768] = folded.astype(BF)
        fifth = jnp.concatenate([two[32:, j * 256:(j + 1) * 256] for j in range(6)], axis=0)
        out_ref[g * 256:(g + 1) * 256, 768:] = dot(spread, fifth).astype(BF)


def merge(*parts):
    return pl.pallas_call(
        merge_kernel,
        out_shape=jax.ShapeDtypeStruct((512, 1024), BF),
        compiler_params=params(),
        cost_estimate=pl.CostEstimate(flops=3 * 10**8, bytes_accessed=3 * 10**6, transcendentals=0),
        name="merge",
    )(*parts)


def combine_kernel(routes_ref, got_ref, out_ref):
    _, match, rank = slot_matches(routes_ref[...])
    inner = iota((EXPERTS * 8, TOK), 0) & 7
    chosen = match & (rank == (inner & 3).astype(F32))
    sides = [mask(chosen & (inner < 4)), mask(chosen & (inner >= 4))]
    chosen = match & (rank == 4.0)
    for j in range(6):
        columns = slice((j % 3) * 256, (j % 3 + 1) * 256)
        total = dot_tn(sides[j // 3], got_ref[:, columns])
        total += dot_tn(mask(chosen & (inner == j)), got_ref[:, 768:])
        out_ref[:, j * 256:(j + 1) * 256] = total.astype(BF)


def combine(routes_t, got):
    return pl.pallas_call(
        combine_kernel,
        out_shape=jax.ShapeDtypeStruct((TOK, D), BF),
        compiler_params=params(),
        cost_estimate=pl.CostEstimate(flops=4 * 10**8, bytes_accessed=2 * 10**6, transcendentals=0),
        name="combine",
    )(routes_t, got)


def per_device(tokens, out_grad, routes, gate_probs, weight_in, weight_out):
    chips = [(i, i ^ 1) for i in range(128)]
    cores = [(0, 1), (1, 0)]
    outer = [4 * i + x for i in range(32) for x in (0, 3)]
    inner = [4 * i + x for i in range(32) for x in (1, 2)]
    halves, everyone = [outer, inner], [outer + inner]
    place = lax.axis_index("expert") & 3
    group = jnp.where((place == 1) | (place == 2), 1, 0).astype(jnp.int32).reshape(1)
    core = lax.axis_index("dp")
    fence = lax.optimization_barrier

    def exchange(rows, groups):
        count = len(groups[0])
        chunked = rows.reshape(count, rows.shape[0] // count, rows.shape[1])
        got = lax.all_to_all(
            chunked, "expert", split_axis=0, concat_axis=0, tiled=True, axis_index_groups=groups
        )
        return got.reshape(rows.shape)

    def gather(weight, axis):
        other = lax.ppermute(weight, "dp", cores)
        first, second = jnp.where(core == 0, weight, other), jnp.where(core == 0, other, weight)
        return jnp.concatenate([first, second], axis=axis)

    routes_t, gates_t = routes.T, gate_probs.T
    send_main, send_last = pack(routes_t, gates_t, tokens, out_grad)
    weight_in, weight_out, send_main = fence((weight_in, weight_out, send_main))
    w1, w2 = gather(weight_in, 0), gather(weight_out, 1)
    own_got = exchange(send_main, halves)
    pair_got = lax.ppermute(own_got, "expert", chips)
    send_last, _ = fence((send_last, own_got[:8, :128] + 1))
    last_got = exchange(send_last, everyone)
    own = expert_rows(False, group, own_got, w1, w2)
    pair_got, _ = fence((pair_got, own[4]))
    pair = expert_rows(False, group, pair_got, w1, w2)
    other_main = lax.ppermute(pair[4], "expert", chips)
    last_got, pair_part = fence((last_got, pair[4]))
    last = expert_rows(True, group, last_got, w1, w2)
    other_last = lax.ppermute(last[5], "expert", chips)
    merged = merge(own[4], other_main, last[4], other_last)
    got = exchange(merged, halves)

    token_all, grad_all, hidden_all, dpre_all = (
        jnp.concatenate([own[i], pair[i], last[i]], axis=0) for i in range(4)
    )

    def half(rows, index):
        return lax.dynamic_slice_in_dim(rows, index * (D // 2), D // 2, axis=1)

    def gradients(index, after):
        tokens, grads, hidden, d_pre, _ = fence((token_all, grad_all, hidden_all, dpre_all, after))
        return dot_tn(half(tokens, index), d_pre), dot_tn(hidden, half(grads, index))

    sent_in, sent_out = (lax.ppermute(v.astype(BF), "dp", cores) for v in gradients(1 - core, other_main))
    kept_in, kept_out = gradients(core, merged)
    grad_in = (kept_in + sent_in.astype(F32)).astype(BF)
    grad_out = (kept_out + sent_out.astype(F32)).astype(BF)
    got, grad_in, grad_out = fence((got, grad_in, grad_out))
    return combine(routes_t, got), grad_in, grad_out


def solution(mesh):
    return jax.shard_map(
        per_device,
        mesh=mesh,
        in_specs=(
            P(("dp", "expert"), None),
            P(("dp", "expert"), None),
            P(("dp", "expert"), None),
            P(("dp", "expert"), None),
            P("dp", "expert"),
            P("expert", "dp"),
        ),
        out_specs=(P(("dp", "expert"), None), P("dp", "expert"), P("expert", "dp")),
        check_vma=False,
    )
```

```python
import functools

import jax
import jax.numpy as jnp
from jax import lax
from jax.experimental import pallas as pl
from jax.experimental.pallas import tpu as pltpu
from jax.sharding import PartitionSpec as P

ROOT_TWO_PI = 0.7978845608
CUBIC = 0.044715
BF = jnp.bfloat16
F32 = jnp.float32
D = 1536
TOK = 128
EXPERTS = 64
HALF = 768
SMALL = pl.CostEstimate(flops=1, bytes_accessed=1, transcendentals=0)


def iota(shape, dim):
    return lax.broadcasted_iota(jnp.int32, shape, dim)


def mask(condition):
    return jnp.where(condition, 1.0, 0.0).astype(BF)


def dot(a, b):
    return jnp.dot(a, b, preferred_element_type=F32)


def dot_nt(a, b):
    return lax.dot_general(a, b, (((1,), (1,)), ((), ())), preferred_element_type=F32)


def dot_tn(a, b):
    return lax.dot_general(a, b, (((0,), (0,)), ((), ())), preferred_element_type=F32)


def whole(shape):
    return pl.BlockSpec(shape, lambda *_: (0,) * len(shape))


def params(mib=40):
    return pltpu.CompilerParams(vmem_limit_bytes=mib * 2**20)


def in_hbm(x):
    return pltpu.with_memory_space_constraint(x, pltpu.HBM)


def hbm_shape(shape):
    return pltpu.HBM(shape, BF)


def after_kernel(x_ref, earlier_ref, out_ref):
    pass


def after(x, earlier):
    anywhere = pl.BlockSpec(memory_space=pl.ANY)
    return pl.pallas_call(
        after_kernel,
        in_specs=[anywhere, anywhere],
        out_specs=anywhere,
        out_shape=jax.ShapeDtypeStruct(x.shape, x.dtype),
        input_output_aliases={0: 0},
        cost_estimate=SMALL,
        name="after",
    )(in_hbm(x), in_hbm(earlier))


def slot_matches(routes_t):
    expert = iota((EXPERTS * 8, TOK), 0) >> 3
    first = routes_t[0:1, :] == expert
    match = first | (routes_t[1:2, :] == expert)
    earlier = mask(iota((TOK, TOK), 0) < iota((TOK, TOK), 1))
    rank = dot(mask(match), earlier)
    return first, match, rank


def pack_kernel(routes_ref, gates_ref, tokens_ref, grads_ref, main_ref, last_ref):
    first, match, rank = slot_matches(routes_ref[...])
    gate = jnp.where(first, gates_ref[0:1, :], gates_ref[1:2, :])
    inner = iota((EXPERTS * 8, TOK), 0) & 7

    def scale_of(chosen):
        return jnp.sum(jnp.where(chosen, gate, 0.0), axis=1, keepdims=True)

    place = jnp.where(inner < 3, inner, inner - 3)
    chosen = match & (rank == place.astype(F32)) & (inner < 6)
    from_tokens, from_grads, scale = mask(chosen & (inner < 3)), mask(chosen & (inner >= 3)), scale_of(chosen)
    for j in range(3):
        columns = slice(j * 384, (j + 1) * 384)
        rows = dot(from_tokens, tokens_ref[:, columns])
        rows += dot(from_grads, grads_ref[:, columns]) * scale
        chosen = match & (rank == float(j))
        rows += dot(mask(chosen & (inner == 6)), tokens_ref[:, 1152:])
        rows += dot(mask(chosen & (inner == 7)), grads_ref[:, 1152:]) * scale_of(chosen)
        main_ref[:, columns] = rows.astype(BF)

    quarter = inner & 3
    chosen = match & (rank == (3 + (quarter & 1)).astype(F32))
    scale = scale_of(chosen)
    rows = jnp.zeros((EXPERTS * 8, 768), F32)
    for j in range(2):
        side = chosen & ((inner >> 2) == j)
        columns = slice(j * 768, (j + 1) * 768)
        rows += dot(mask(side & (quarter < 2)), tokens_ref[:, columns])
        rows += dot(mask(side & (quarter >= 2)), grads_ref[:, columns]) * scale
    last = rows.astype(BF)
    last_ref[0:512, :] = last
    last_ref[512:1024, :] = last


def pack(routes_t, gates_t, tokens, out_grad):
    return pl.pallas_call(
        pack_kernel,
        out_shape=(
            hbm_shape((512, 1152)),
            hbm_shape((1024, 768)),
        ),
        compiler_params=params(),
        cost_estimate=SMALL,
        name="pack",
    )(routes_t, gates_t, tokens, out_grad)


def unpack(last, got_ref, token_ref, grad_ref):
    row, column = iota((256, 256), 0), iota((256, 256), 1)
    move = mask(column == ((row & 31) << 3) + (row >> 5))
    for g in range(got_ref.shape[0] // 256):
        rows = dot(move, got_ref[g * 256:(g + 1) * 256, :]).astype(BF)
        if last:
            for j in range(2):
                columns = slice(j * 768, (j + 1) * 768)
                token_ref[g * 64:(g + 1) * 64, columns] = rows[j * 128:j * 128 + 64]
                grad_ref[g * 64:(g + 1) * 64, columns] = rows[j * 128 + 64:j * 128 + 128]
        else:
            token_ref[g * 96:(g + 1) * 96, :1152] = rows[:96]
            grad_ref[g * 96:(g + 1) * 96, :1152] = rows[96:192]
            for j in range(3):
                target = slice(g * 96 + j * 32, g * 96 + (j + 1) * 32)
                token_ref[target, 1152:] = rows[192:224, j * 384:(j + 1) * 384]
                grad_ref[target, 1152:] = rows[224:256, j * 384:(j + 1) * 384]


def expert_kernel(last, flags_ref, earlier_ref, got_ref, w1_mine, w1_other, w2_mine, w2_other, mine_ref, send_ref, *rest):
    *part_refs, token, grad, total_mine, total_other = rest
    step = pl.program_id(0)
    low, high = slice(0, HALF), slice(HALF, D)
    first = flags_ref[0] == 0

    def both_orders(run):
        pl.when(first)(lambda: run(low, high))
        pl.when(jnp.logical_not(first))(lambda: run(high, low))

    @pl.when(step == 0)
    def _():
        unpack(last, got_ref, token, grad)

        def split(own, other):
            mine_ref[:, low] = token[:, own]
            mine_ref[:, high] = grad[:, own]
            send_ref[:, low] = token[:, other]
            send_ref[:, high] = grad[:, other]

        both_orders(split)

    pre = dot(mine_ref[:, low], w1_mine[...]) + dot(send_ref[:, low], w1_other[...])
    back = dot_nt(mine_ref[:, high], w2_mine[...]) + dot_nt(send_ref[:, high], w2_other[...])
    square = pre * pre
    th = jnp.tanh(ROOT_TWO_PI * (pre + CUBIC * square * pre))
    half = 0.5 * (1.0 + th)
    hidden = (pre * half).astype(BF)
    slope = half + 0.5 * pre * (1.0 - th * th) * ROOT_TWO_PI * (1.0 + 3.0 * CUBIC * square)
    d_pre = (back * slope).astype(BF)
    for k in range(2):
        @pl.when(step == k)
        def _(k=k):
            send_ref[:, (2 + k) * HALF:(3 + k) * HALF] = hidden
            send_ref[:, (4 + k) * HALF:(5 + k) * HALF] = d_pre
    term_mine, term_other = dot_nt(d_pre, w1_mine[...]), dot_nt(d_pre, w1_other[...])

    @pl.when(step == 0)
    def _():
        total_mine[...] = term_mine
        total_other[...] = term_other

    @pl.when(step == 1)
    def _():
        total_mine[...] += term_mine
        total_other[...] += term_other

        def finish(own, other):
            for columns, total in ((own, total_mine), (other, total_other)):
                if last:
                    for k, part_ref in enumerate(part_refs):
                        group = flags_ref[1] if k == 0 else 1 - flags_ref[1]
                        rows = pl.ds(pl.multiple_of(group * 128, 128), 128)
                        part_ref[:, columns] = total[rows, :].astype(BF)
                else:
                    part_refs[0][:, columns] = total[...].astype(BF)

        both_orders(finish)


def expert_rows(last, flags, earlier, got, weights):
    rows = 256 if last else 192
    parts = [(128, D)] * 2 if last else [(192, D)]
    first = pl.BlockSpec((HALF, HALF), lambda h: (0, h))
    second = pl.BlockSpec((HALF, HALF), lambda h: (h, 0))
    outs = [(rows, D), (rows, 3 * D), *parts]
    return pl.pallas_call(
        functools.partial(expert_kernel, last),
        grid=(2,),
        in_specs=[
            pl.BlockSpec(memory_space=pltpu.SMEM),
            pl.BlockSpec(memory_space=pl.ANY),
            whole(got.shape),
            first, first, second, second,
        ],
        out_specs=tuple(whole(shape) for shape in outs),
        out_shape=tuple(hbm_shape(shape) for shape in outs),
        scratch_shapes=[pltpu.VMEM((rows, D), BF)] * 2 + [pltpu.VMEM((rows, HALF), F32)] * 2,
        compiler_params=params(32),
        cost_estimate=SMALL,
        name="expert_last" if last else "expert_main",
    )(flags, in_hbm(earlier), got, *weights)


def weight_grads_kernel(*refs):
    in_ref, out_ref = refs[-2:]
    first = second = None
    for i in range(0, 24, 4):
        token_ref, grad_ref, hidden_ref, dpre_ref = refs[i:i + 4]
        a, b = dot_tn(token_ref[...], dpre_ref[...]), dot_tn(hidden_ref[...], grad_ref[...])
        first, second = (a, b) if first is None else (first + a, second + b)
    in_ref[...] = first.astype(BF)
    out_ref[...] = second.astype(BF)


def weight_grads(sets):
    specs, operands = [], []

    def take(x, block, moves):
        operands.append(in_hbm(x))
        index = (lambda h: (0, block + h)) if moves else (lambda h: (0, block))
        specs.append(pl.BlockSpec((x.shape[0], HALF), index))

    for mine, send, received in sets:
        for near, far in ((mine, send), (received, received)):
            take(near, 0, False)
            take(near, 1, False)
            take(far, 2, True)
            take(far, 4, True)
    return pl.pallas_call(
        weight_grads_kernel,
        grid=(2,),
        in_specs=specs,
        out_specs=(
            pl.BlockSpec((HALF, HALF), lambda h: (0, h)),
            pl.BlockSpec((HALF, HALF), lambda h: (h, 0)),
        ),
        out_shape=(hbm_shape((HALF, D)), hbm_shape((D, HALF))),
        compiler_params=params(48),
        cost_estimate=SMALL,
        name="weight_grads",
    )(*operands)


def merge_kernel(main_a, main_b, last_a, last_b, out_ref):
    row, column = iota((256, 128), 0), iota((256, 128), 1)
    target = ((column & 31) << 3) + (column >> 5)
    row6, column6 = iota((256, 192), 0), iota((256, 192), 1)
    spread = mask(row6 == ((column6 & 31) << 3) + (column6 >> 5))
    for g in range(2):
        a, b = slice(g * 96, (g + 1) * 96), slice(g * 64, (g + 1) * 64)
        three = (main_a[a, :].astype(F32) + main_b[a, :].astype(F32)).astype(BF)
        two = (last_a[b, :].astype(F32) + last_b[b, :].astype(F32)).astype(BF)
        four = jnp.concatenate([three, two[:32]], axis=0)
        folded = dot(mask(row == target), four[:, :768]) + dot(mask(row == target + 4), four[:, 768:])
        out_ref[g * 256:(g + 1) * 256, :768] = folded.astype(BF)
        fifth = jnp.concatenate([two[32:, j * 256:(j + 1) * 256] for j in range(6)], axis=0)
        out_ref[g * 256:(g + 1) * 256, 768:] = dot(spread, fifth).astype(BF)


def merge(*parts):
    return pl.pallas_call(
        merge_kernel,
        out_shape=hbm_shape((512, 1024)),
        compiler_params=params(),
        cost_estimate=SMALL,
        name="merge",
    )(in_hbm(parts[0]), parts[1], in_hbm(parts[2]), parts[3])


def combine_kernel(routes_ref, got_ref, earlier_ref, out_ref):
    _, match, rank = slot_matches(routes_ref[...])
    inner = iota((EXPERTS * 8, TOK), 0) & 7
    chosen = match & (rank == (inner & 3).astype(F32))
    sides = [mask(chosen & (inner < 4)), mask(chosen & (inner >= 4))]
    chosen = match & (rank == 4.0)
    for j in range(6):
        columns = slice((j % 3) * 256, (j % 3 + 1) * 256)
        total = dot_tn(sides[j // 3], got_ref[:, columns])
        total += dot_tn(mask(chosen & (inner == j)), got_ref[:, 768:])
        out_ref[:, j * 256:(j + 1) * 256] = total.astype(BF)


def combine(routes_t, got, earlier):
    return pl.pallas_call(
        combine_kernel,
        in_specs=[whole(routes_t.shape), whole(got.shape), pl.BlockSpec(memory_space=pl.ANY)],
        out_specs=whole((TOK, D)),
        out_shape=jax.ShapeDtypeStruct((TOK, D), BF),
        compiler_params=params(),
        cost_estimate=SMALL,
        name="combine",
    )(routes_t, got, in_hbm(earlier))


def per_device(tokens, out_grad, routes, gate_probs, weight_in, weight_out):
    chips = [(i, i ^ 1) for i in range(128)]
    cores = [(0, 1), (1, 0)]
    outer = [4 * i + x for i in range(32) for x in (0, 3)]
    inner = [4 * i + x for i in range(32) for x in (1, 2)]
    halves, everyone = [outer, inner], [outer + inner]
    place = lax.axis_index("expert") & 3
    group = jnp.where((place == 1) | (place == 2), 1, 0)
    flags = jnp.stack([lax.axis_index("dp"), group]).astype(jnp.int32)

    def exchange(rows, groups):
        count = len(groups[0])
        chunked = rows.reshape(count, rows.shape[0] // count, rows.shape[1])
        got = lax.all_to_all(
            chunked, "expert", split_axis=0, concat_axis=0, tiled=True, axis_index_groups=groups
        )
        return got.reshape(rows.shape)

    def to_other_core(x):
        return lax.ppermute(x, "dp", cores)

    weights = (weight_in, to_other_core(weight_in), weight_out, to_other_core(weight_out))
    routes_t, gates_t = routes.T, gate_probs.T
    send_main, send_last = pack(routes_t, gates_t, tokens, out_grad)
    own_got = exchange(send_main, halves)
    pair_got = lax.ppermute(own_got, "expert", chips)
    own_mine, own_send, own_part = expert_rows(False, flags, send_main, own_got, weights)
    last_got = exchange(send_last, everyone)
    pair_mine, pair_send, pair_part = expert_rows(False, flags, own_part, pair_got, weights)
    other_main = lax.ppermute(pair_part, "expert", chips)
    last_mine, last_send, last_part, last_away = expert_rows(True, flags, pair_part, last_got, weights)
    other_last = lax.ppermute(last_away, "expert", chips)
    merged = merge(own_part, other_main, last_part, other_last)
    got = exchange(merged, halves)
    grad_in, grad_out = weight_grads([
        (own_mine, own_send, to_other_core(own_send)),
        (pair_mine, pair_send, to_other_core(pair_send)),
        (after(last_mine, merged), last_send, to_other_core(last_send)),
    ])
    return combine(routes_t, got, grad_in), grad_in, grad_out


def solution(mesh):
    return jax.shard_map(
        per_device,
        mesh=mesh,
        in_specs=(
            P(("dp", "expert"), None),
            P(("dp", "expert"), None),
            P(("dp", "expert"), None),
            P(("dp", "expert"), None),
            P("dp", "expert"),
            P("expert", "dp"),
        ),
        out_specs=(P(("dp", "expert"), None), P("dp", "expert"), P("expert", "dp")),
        check_vma=False,
    )
```

```python
import functools

import jax
import jax.numpy as jnp
from jax import lax
from jax.experimental import pallas as pl
from jax.experimental.pallas import tpu as pltpu
from jax.sharding import PartitionSpec as P

ROOT_TWO_PI = 0.7978845608
CUBIC = 0.044715
BF = jnp.bfloat16
F32 = jnp.float32
D = 1536
TOK = 128
EXPERTS = 64
HALF = 768
LARGE = pl.CostEstimate(flops=10**11, bytes_accessed=10**8, transcendentals=0)
SMALL = pl.CostEstimate(flops=1, bytes_accessed=1, transcendentals=0)


def iota(shape, dim):
    return lax.broadcasted_iota(jnp.int32, shape, dim)


def mask(condition):
    return jnp.where(condition, 1.0, 0.0).astype(BF)


def dot(a, b):
    return jnp.dot(a, b, preferred_element_type=F32)


def dot_nt(a, b):
    return lax.dot_general(a, b, (((1,), (1,)), ((), ())), preferred_element_type=F32)


def dot_tn(a, b):
    return lax.dot_general(a, b, (((0,), (0,)), ((), ())), preferred_element_type=F32)


def whole(shape):
    return pl.BlockSpec(shape, lambda *_: (0,) * len(shape))


def params(mib=40):
    return pltpu.CompilerParams(vmem_limit_bytes=mib * 2**20)


def in_hbm(x):
    return pltpu.with_memory_space_constraint(x, pltpu.HBM)


def hbm_shape(shape):
    return pltpu.HBM(shape, BF)


def after_kernel(x_ref, earlier_ref, out_ref):
    pass


def after(x, earlier):
    anywhere = pl.BlockSpec(memory_space=pl.ANY)
    return pl.pallas_call(
        after_kernel,
        in_specs=[anywhere, anywhere],
        out_specs=anywhere,
        out_shape=jax.ShapeDtypeStruct(x.shape, x.dtype),
        input_output_aliases={0: 0},
        cost_estimate=SMALL,
        name="after",
    )(in_hbm(x), in_hbm(earlier))


def slot_matches(routes_t):
    expert = iota((EXPERTS * 8, TOK), 0) >> 3
    first = routes_t[0:1, :] == expert
    match = first | (routes_t[1:2, :] == expert)
    earlier = mask(iota((TOK, TOK), 0) < iota((TOK, TOK), 1))
    rank = dot(mask(match), earlier)
    return first, match, rank


def pack_kernel(routes_ref, gates_ref, tokens_ref, grads_ref, main_ref, last_ref):
    first, match, rank = slot_matches(routes_ref[...])
    gate = jnp.where(first, gates_ref[0:1, :], gates_ref[1:2, :])
    inner = iota((EXPERTS * 8, TOK), 0) & 7

    def scale_of(chosen):
        return jnp.sum(jnp.where(chosen, gate, 0.0), axis=1, keepdims=True)

    place = jnp.where(inner < 3, inner, inner - 3)
    chosen = match & (rank == place.astype(F32)) & (inner < 6)
    from_tokens, from_grads, scale = mask(chosen & (inner < 3)), mask(chosen & (inner >= 3)), scale_of(chosen)
    for j in range(3):
        columns = slice(j * 384, (j + 1) * 384)
        rows = dot(from_tokens, tokens_ref[:, columns])
        rows += dot(from_grads, grads_ref[:, columns]) * scale
        chosen = match & (rank == float(j))
        rows += dot(mask(chosen & (inner == 6)), tokens_ref[:, 1152:])
        rows += dot(mask(chosen & (inner == 7)), grads_ref[:, 1152:]) * scale_of(chosen)
        main_ref[:, columns] = rows.astype(BF)

    quarter = inner & 3
    chosen = match & (rank == (3 + (quarter & 1)).astype(F32))
    scale = scale_of(chosen)
    rows = jnp.zeros((EXPERTS * 8, 768), F32)
    for j in range(2):
        side = chosen & ((inner >> 2) == j)
        columns = slice(j * 768, (j + 1) * 768)
        rows += dot(mask(side & (quarter < 2)), tokens_ref[:, columns])
        rows += dot(mask(side & (quarter >= 2)), grads_ref[:, columns]) * scale
    last = rows.astype(BF)
    last_ref[0:512, :] = last
    last_ref[512:1024, :] = last


def pack(routes_t, gates_t, tokens, out_grad):
    return pl.pallas_call(
        pack_kernel,
        out_shape=(
            hbm_shape((512, 1152)),
            hbm_shape((1024, 768)),
        ),
        compiler_params=params(),
        cost_estimate=SMALL,
        name="pack",
    )(*map(in_hbm, (routes_t, gates_t, tokens, out_grad)))


def unpack(last, got_ref, token_ref, grad_ref):
    row, column = iota((256, 256), 0), iota((256, 256), 1)
    move = mask(column == ((row & 31) << 3) + (row >> 5))
    for g in range(got_ref.shape[0] // 256):
        rows = dot(move, got_ref[g * 256:(g + 1) * 256, :]).astype(BF)
        if last:
            for j in range(2):
                columns = slice(j * 768, (j + 1) * 768)
                token_ref[g * 64:(g + 1) * 64, columns] = rows[j * 128:j * 128 + 64]
                grad_ref[g * 64:(g + 1) * 64, columns] = rows[j * 128 + 64:j * 128 + 128]
        else:
            token_ref[g * 96:(g + 1) * 96, :1152] = rows[:96]
            grad_ref[g * 96:(g + 1) * 96, :1152] = rows[96:192]
            for j in range(3):
                target = slice(g * 96 + j * 32, g * 96 + (j + 1) * 32)
                token_ref[target, 1152:] = rows[192:224, j * 384:(j + 1) * 384]
                grad_ref[target, 1152:] = rows[224:256, j * 384:(j + 1) * 384]


def expert_kernel(last, flags_ref, earlier_ref, got_ref, in_mine, in_other, out_mine, out_other, *rest):
    count = 4 if last else 3
    mine_out, send_out, *part_outs = rest[:count]
    w1_mine, w1_other, w2_mine, w2_other, token, grad, mine, send, units_out, *parts, loads, stores = rest[count:]
    low, high = pl.ds(0, HALF), pl.ds(HALF, HALF)
    first = flags_ref[0] == 0
    weights = ((in_mine, w1_mine), (in_other, w1_other), (out_mine, w2_mine), (out_other, w2_other))
    arrivals = []
    for source, target in weights:
        half = source.shape[0] // 2
        for k in range(2):
            rows = pl.ds(k * half, half)
            arrivals.append(pltpu.make_async_copy(source.at[rows, :], target.at[rows, :], loads.at[len(arrivals)]))
    for k in (0, 1, 2, 3, 4, 6, 5, 7):
        arrivals[k].start()

    unpack(last, got_ref, token, grad)

    def both_orders(run):
        pl.when(first)(lambda: run(low, high))
        pl.when(jnp.logical_not(first))(lambda: run(high, low))

    def split(own, other):
        mine[:, low] = token[:, own]
        mine[:, high] = grad[:, own]
        send[:, low] = token[:, other]
        send[:, high] = grad[:, other]

    both_orders(split)
    departures = []

    def depart(source, target):
        departures.append(pltpu.make_async_copy(source, target, stores.at[len(departures)]))
        departures[-1].start()

    depart(mine, mine_out)
    depart(send, send_out.at[:, pl.ds(0, D)])
    pre = None
    for k, (rows, w1) in enumerate(((mine, w1_mine), (mine, w1_mine), (send, w1_other), (send, w1_other))):
        arrivals[k].wait()
        part = pl.ds((k % 2) * (HALF // 2), HALF // 2)
        term = dot(rows[:, part], w1[part, :])
        pre = term if pre is None else pre + term
    for k in range(2):
        units = slice(k * HALF, (k + 1) * HALF)
        arrivals[4 + k].wait()
        arrivals[6 + k].wait()
        back = dot_nt(mine[:, high], w2_mine[units, :]) + dot_nt(send[:, high], w2_other[units, :])
        value = pre[:, units]
        square = value * value
        th = jnp.tanh(ROOT_TWO_PI * (value + CUBIC * square * value))
        half = 0.5 * (1.0 + th)
        slope = half + 0.5 * value * (1.0 - th * th) * ROOT_TWO_PI * (1.0 + 3.0 * CUBIC * square)
        units_out[:, k * HALF:(k + 1) * HALF] = (value * half).astype(BF)
        units_out[:, (2 + k) * HALF:(3 + k) * HALF] = (back * slope).astype(BF)
    depart(units_out, send_out.at[:, pl.ds(D, 2 * D)])
    d_pre = units_out[:, D:]
    part_mine, part_other = dot_nt(d_pre, w1_mine[...]).astype(BF), dot_nt(d_pre, w1_other[...]).astype(BF)

    def finish(own, other):
        for columns, part in ((own, part_mine), (other, part_other)):
            if last:
                kept, away = parts

                @pl.when(flags_ref[1] == 0)
                def _():
                    kept[:, columns], away[:, columns] = part[:128], part[128:]

                @pl.when(flags_ref[1] != 0)
                def _():
                    kept[:, columns], away[:, columns] = part[128:], part[:128]
            else:
                parts[0][:, columns] = part

    both_orders(finish)
    for part, out in zip(parts, part_outs):
        depart(part, out)
    for copy in departures:
        copy.wait()


def expert_rows(last, flags, earlier, got, weights, cost=SMALL):
    rows = 256 if last else 192
    parts = [(128, D)] * 2 if last else [(192, D)]
    outs = [(rows, D), (rows, 3 * D), *parts]
    anywhere = pl.BlockSpec(memory_space=pl.ANY)
    buffers = [(HALF, D)] * 2 + [(D, HALF)] * 2 + [(rows, D)] * 4 + [(rows, 2 * D)] + parts
    return pl.pallas_call(
        functools.partial(expert_kernel, last),
        in_specs=[
            pl.BlockSpec(memory_space=pltpu.SMEM), anywhere, whole(got.shape), *[anywhere] * 4
        ],
        out_specs=(anywhere,) * len(outs),
        out_shape=tuple(hbm_shape(shape) for shape in outs),
        scratch_shapes=[
            *(pltpu.VMEM(shape, BF) for shape in buffers),
            pltpu.SemaphoreType.DMA((8,)),
            pltpu.SemaphoreType.DMA((5,)),
        ],
        compiler_params=params(40),
        cost_estimate=cost,
        name="expert_last" if last else "expert_main",
    )(flags, in_hbm(earlier), got, *(in_hbm(weight) for weight in weights))


def weight_grads_kernel(*refs):
    in_ref, out_ref = refs[-2:]
    first = second = None
    for i in range(0, 24, 4):
        token_ref, grad_ref, hidden_ref, dpre_ref = refs[i:i + 4]
        a, b = dot_tn(token_ref[...], dpre_ref[...]), dot_tn(hidden_ref[...], grad_ref[...])
        first, second = (a, b) if first is None else (first + a, second + b)
    in_ref[...] = first.astype(BF)
    out_ref[...] = second.astype(BF)


def weight_grads(sets):
    specs, operands = [], []

    def take(x, block, moves):
        operands.append(in_hbm(x))
        index = (lambda h: (0, block + h)) if moves else (lambda h: (0, block))
        specs.append(pl.BlockSpec((x.shape[0], HALF), index))

    for mine, send, received in sets:
        for near, far in ((mine, send), (received, received)):
            take(near, 0, False)
            take(near, 1, False)
            take(far, 2, True)
            take(far, 4, True)
    return pl.pallas_call(
        weight_grads_kernel,
        grid=(2,),
        in_specs=specs,
        out_specs=(
            pl.BlockSpec((HALF, HALF), lambda h: (0, h)),
            pl.BlockSpec((HALF, HALF), lambda h: (h, 0)),
        ),
        out_shape=(hbm_shape((HALF, D)), hbm_shape((D, HALF))),
        compiler_params=params(48),
        cost_estimate=SMALL,
        name="weight_grads",
    )(*operands)


def merge_kernel(main_a, main_b, last_a, last_b, out_ref):
    row, column = iota((256, 128), 0), iota((256, 128), 1)
    target = ((column & 31) << 3) + (column >> 5)
    row6, column6 = iota((256, 192), 0), iota((256, 192), 1)
    spread = mask(row6 == ((column6 & 31) << 3) + (column6 >> 5))
    for g in range(2):
        a, b = slice(g * 96, (g + 1) * 96), slice(g * 64, (g + 1) * 64)
        three = (main_a[a, :].astype(F32) + main_b[a, :].astype(F32)).astype(BF)
        two = (last_a[b, :].astype(F32) + last_b[b, :].astype(F32)).astype(BF)
        four = jnp.concatenate([three, two[:32]], axis=0)
        folded = dot(mask(row == target), four[:, :768]) + dot(mask(row == target + 4), four[:, 768:])
        out_ref[g * 256:(g + 1) * 256, :768] = folded.astype(BF)
        fifth = jnp.concatenate([two[32:, j * 256:(j + 1) * 256] for j in range(6)], axis=0)
        out_ref[g * 256:(g + 1) * 256, 768:] = dot(spread, fifth).astype(BF)


def merge(*parts):
    return pl.pallas_call(
        merge_kernel,
        out_shape=hbm_shape((512, 1024)),
        compiler_params=params(),
        cost_estimate=SMALL,
        name="merge",
    )(in_hbm(parts[0]), parts[1], in_hbm(parts[2]), parts[3])


def combine_kernel(routes_ref, got_ref, earlier_ref, out_ref):
    _, match, rank = slot_matches(routes_ref[...])
    inner = iota((EXPERTS * 8, TOK), 0) & 7
    chosen = match & (rank == (inner & 3).astype(F32))
    sides = [mask(chosen & (inner < 4)), mask(chosen & (inner >= 4))]
    chosen = match & (rank == 4.0)
    for j in range(6):
        columns = slice((j % 3) * 256, (j % 3 + 1) * 256)
        total = dot_tn(sides[j // 3], got_ref[:, columns])
        total += dot_tn(mask(chosen & (inner == j)), got_ref[:, 768:])
        out_ref[:, j * 256:(j + 1) * 256] = total.astype(BF)


def combine(routes_t, got, earlier):
    return pl.pallas_call(
        combine_kernel,
        in_specs=[whole(routes_t.shape), whole(got.shape), pl.BlockSpec(memory_space=pl.ANY)],
        out_specs=whole((TOK, D)),
        out_shape=jax.ShapeDtypeStruct((TOK, D), BF),
        compiler_params=params(),
        cost_estimate=SMALL,
        name="combine",
    )(routes_t, got, in_hbm(earlier))


def per_device(tokens, out_grad, routes, gate_probs, weight_in, weight_out):
    chips = [(i, i ^ 1) for i in range(128)]
    cores = [(0, 1), (1, 0)]
    outer = [4 * i + x for i in range(32) for x in (0, 3)]
    inner = [4 * i + x for i in range(32) for x in (1, 2)]
    halves, everyone = [outer, inner], [outer + inner]
    place = lax.axis_index("expert") & 3
    group = jnp.where((place == 1) | (place == 2), 1, 0)
    flags = jnp.stack([lax.axis_index("dp"), group]).astype(jnp.int32)

    def exchange(rows, groups):
        count = len(groups[0])
        chunked = rows.reshape(count, rows.shape[0] // count, rows.shape[1])
        got = lax.all_to_all(
            chunked, "expert", split_axis=0, concat_axis=0, tiled=True, axis_index_groups=groups
        )
        return got.reshape(rows.shape)

    def to_other_core(x):
        return lax.ppermute(x, "dp", cores)

    weights = (weight_in, to_other_core(weight_in), weight_out, to_other_core(weight_out))
    routes_t, gates_t = routes.T, gate_probs.T
    send_main, send_last = pack(routes_t, gates_t, tokens, out_grad)
    own_got = exchange(send_main, halves)
    pair_got = lax.ppermute(own_got, "expert", chips)
    own_mine, own_send, own_part = expert_rows(False, flags, send_main, own_got, weights)
    last_got = exchange(send_last, everyone)
    pair_mine, pair_send, pair_part = expert_rows(False, flags, own_part, pair_got, weights, LARGE)
    other_main = lax.ppermute(pair_part, "expert", chips)
    last_mine, last_send, last_part, last_away = expert_rows(True, flags, pair_part, last_got, weights)
    other_last = lax.ppermute(last_away, "expert", chips)
    merged = merge(own_part, other_main, last_part, other_last)
    got = exchange(merged, halves)
    grad_in, grad_out = weight_grads([
        (own_mine, own_send, to_other_core(own_send)),
        (pair_mine, pair_send, to_other_core(pair_send)),
        (after(last_mine, merged), last_send, to_other_core(last_send)),
    ])
    return combine(routes_t, got, grad_in), grad_in, grad_out


def solution(mesh):
    return jax.shard_map(
        per_device,
        mesh=mesh,
        in_specs=(
            P(("dp", "expert"), None),
            P(("dp", "expert"), None),
            P(("dp", "expert"), None),
            P(("dp", "expert"), None),
            P("dp", "expert"),
            P("expert", "dp"),
        ),
        out_specs=(P(("dp", "expert"), None), P("dp", "expert"), P("expert", "dp")),
        check_vma=False,
    )
```

```python
import functools

import jax
import jax.numpy as jnp
from jax import lax
from jax.experimental import pallas as pl
from jax.experimental.pallas import tpu as pltpu
from jax.sharding import PartitionSpec as P

ROOT_TWO_PI = 0.7978845608
CUBIC = 0.044715
BF = jnp.bfloat16
F32 = jnp.float32
D = 1536
TOK = 128
EXPERTS = 64
HALF = 768
LARGE = pl.CostEstimate(flops=10**11, bytes_accessed=10**8, transcendentals=0)
SMALL = pl.CostEstimate(flops=1, bytes_accessed=1, transcendentals=0)


def iota(shape, dim):
    return lax.broadcasted_iota(jnp.int32, shape, dim)


def mask(condition):
    return jnp.where(condition, 1.0, 0.0).astype(BF)


def dot(a, b):
    return jnp.dot(a, b, preferred_element_type=F32)


def dot_nt(a, b):
    return lax.dot_general(a, b, (((1,), (1,)), ((), ())), preferred_element_type=F32)


def dot_tn(a, b):
    return lax.dot_general(a, b, (((0,), (0,)), ((), ())), preferred_element_type=F32)


def whole(shape):
    return pl.BlockSpec(shape, lambda *_: (0,) * len(shape))


def params(mib=40):
    return pltpu.CompilerParams(vmem_limit_bytes=mib * 2**20)


def in_hbm(x):
    return pltpu.with_memory_space_constraint(x, pltpu.HBM)


def hbm_shape(shape):
    return pltpu.HBM(shape, BF)


def after_kernel(x_ref, earlier_ref, out_ref):
    pass


def after(x, earlier):
    anywhere = pl.BlockSpec(memory_space=pl.ANY)
    return pl.pallas_call(
        after_kernel,
        in_specs=[anywhere, anywhere],
        out_specs=anywhere,
        out_shape=jax.ShapeDtypeStruct(x.shape, x.dtype),
        input_output_aliases={0: 0},
        cost_estimate=SMALL,
        name="after",
    )(in_hbm(x), in_hbm(earlier))


def slot_matches(routes_t):
    expert = iota((EXPERTS * 8, TOK), 0) >> 3
    first = routes_t[0:1, :] == expert
    match = first | (routes_t[1:2, :] == expert)
    earlier = mask(iota((TOK, TOK), 0) < iota((TOK, TOK), 1))
    rank = dot(mask(match), earlier)
    return first, match, rank


def pack_main_kernel(routes_ref, gates_ref, tokens_ref, grads_ref, main_ref):
    first, match, rank = slot_matches(routes_ref[...])
    gate = jnp.where(first, gates_ref[0:1, :], gates_ref[1:2, :])
    inner = iota((EXPERTS * 8, TOK), 0) & 7
    place = jnp.where(inner < 3, inner, inner - 3)
    chosen = match & (rank == place.astype(F32)) & (inner < 6)
    from_tokens, from_grads = mask(chosen & (inner < 3)), mask(chosen & (inner >= 3))
    token_tail, grad_tail = tokens_ref[:, 1152:], grads_ref[:, 1152:]
    for j in range(3):
        columns = slice(j * 384, (j + 1) * 384)
        tail = match & (rank == float(j)) & (inner >= 6)
        scale = jnp.sum(jnp.where(chosen | tail, gate, 0.0), axis=1, keepdims=True)
        rows = dot(
            jnp.concatenate([from_tokens, mask(tail & (inner == 6))], axis=1),
            jnp.concatenate([tokens_ref[:, columns], token_tail], axis=0),
        )
        rows += scale * dot(
            jnp.concatenate([from_grads, mask(tail & (inner == 7))], axis=1),
            jnp.concatenate([grads_ref[:, columns], grad_tail], axis=0),
        )
        main_ref[:, columns] = rows.astype(BF)


def pack_last_kernel(routes_ref, gates_ref, tokens_ref, grads_ref, last_ref):
    first, match, rank = slot_matches(routes_ref[...])
    gate = jnp.where(first, gates_ref[0:1, :], gates_ref[1:2, :])
    inner = iota((EXPERTS * 8, TOK), 0) & 7
    quarter = inner & 3
    chosen = match & (rank == (3 + (quarter & 1)).astype(F32))
    scale = jnp.sum(jnp.where(chosen, gate, 0.0), axis=1, keepdims=True)
    rows = jnp.zeros((EXPERTS * 8, 768), F32)
    for j in range(2):
        side = chosen & ((inner >> 2) == j)
        columns = slice(j * 768, (j + 1) * 768)
        rows += dot(mask(side & (quarter < 2)), tokens_ref[:, columns])
        rows += dot(mask(side & (quarter >= 2)), grads_ref[:, columns]) * scale
    last = rows.astype(BF)
    last_ref[0:512, :] = last
    last_ref[512:1024, :] = last


def pack(last, *operands):
    return pl.pallas_call(
        pack_last_kernel if last else pack_main_kernel,
        out_shape=hbm_shape((1024, 768) if last else (512, 1152)),
        compiler_params=params(),
        cost_estimate=SMALL,
        name="pack_last" if last else "pack_main",
    )(*map(in_hbm, operands))


def unpack(last, got_ref, token_ref, grad_ref):
    row, column = iota((256, 256), 0), iota((256, 256), 1)
    move = mask(column == ((row & 31) << 3) + (row >> 5))
    for g in range(got_ref.shape[0] // 256):
        rows = dot(move, got_ref[g * 256:(g + 1) * 256, :]).astype(BF)
        if last:
            for j in range(2):
                columns = slice(j * 768, (j + 1) * 768)
                token_ref[g * 64:(g + 1) * 64, columns] = rows[j * 128:j * 128 + 64]
                grad_ref[g * 64:(g + 1) * 64, columns] = rows[j * 128 + 64:j * 128 + 128]
        else:
            token_ref[g * 96:(g + 1) * 96, :1152] = rows[:96]
            grad_ref[g * 96:(g + 1) * 96, :1152] = rows[96:192]
            for j in range(3):
                target = slice(g * 96 + j * 32, g * 96 + (j + 1) * 32)
                token_ref[target, 1152:] = rows[192:224, j * 384:(j + 1) * 384]
                grad_ref[target, 1152:] = rows[224:256, j * 384:(j + 1) * 384]


def expert_kernel(last, flags_ref, earlier_ref, got_ref, in_mine, in_other, out_mine, out_other, *rest):
    count = 4 if last else 3
    mine_out, send_out, *part_outs = rest[:count]
    w1_mine, w1_other, w2_mine, w2_other, got, token, grad, mine, send, units_out, *parts, loads, stores = rest[count:]
    low, high = pl.ds(0, HALF), pl.ds(HALF, HALF)
    first = flags_ref[0] == 0
    weights = ((in_mine, w1_mine), (in_other, w1_other), (out_mine, w2_mine), (out_other, w2_other))
    arrivals = []
    for source, target in weights:
        half = source.shape[0] // 2
        for k in range(2):
            rows = pl.ds(k * half, half)
            arrivals.append(pltpu.make_async_copy(source.at[rows, :], target.at[rows, :], loads.at[len(arrivals)]))
    got_here = pltpu.make_async_copy(got_ref, got, loads.at[8])
    got_here.start()
    for k in (0, 1, 2, 3, 4, 6, 5, 7):
        arrivals[k].start()
    got_here.wait()
    unpack(last, got, token, grad)

    def both_orders(run):
        pl.when(first)(lambda: run(low, high))
        pl.when(jnp.logical_not(first))(lambda: run(high, low))

    def split(own, other):
        mine[:, low] = token[:, own]
        mine[:, high] = grad[:, own]
        send[:, low] = token[:, other]
        send[:, high] = grad[:, other]

    both_orders(split)
    departures = []

    def depart(source, target):
        departures.append(pltpu.make_async_copy(source, target, stores.at[len(departures)]))
        departures[-1].start()

    pre = part_mine = part_other = None
    for k, (rows, w1) in enumerate(((mine, w1_mine), (mine, w1_mine), (send, w1_other), (send, w1_other))):
        arrivals[k].wait()
        part = pl.ds((k % 2) * (HALF // 2), HALF // 2)
        term = dot(rows[:, part], w1[part, :])
        pre = term if pre is None else pre + term
    for k in range(2):
        units = slice(k * HALF, (k + 1) * HALF)
        arrivals[4 + k].wait()
        arrivals[6 + k].wait()
        back = dot_nt(mine[:, high], w2_mine[units, :]) + dot_nt(send[:, high], w2_other[units, :])
        value = pre[:, units]
        square = value * value
        th = jnp.tanh(ROOT_TWO_PI * (value + CUBIC * square * value))
        half = 0.5 * (1.0 + th)
        slope = half + 0.5 * value * (1.0 - th * th) * ROOT_TWO_PI * (1.0 + 3.0 * CUBIC * square)
        d_pre = (back * slope).astype(BF)
        units_out[:, k * HALF:(k + 1) * HALF] = (value * half).astype(BF)
        units_out[:, (2 + k) * HALF:(3 + k) * HALF] = d_pre
        if k == 1:
            depart(mine, mine_out)
            depart(send, send_out.at[:, pl.ds(0, D)])
            depart(units_out, send_out.at[:, pl.ds(D, 2 * D)])
        terms = dot_nt(d_pre, w1_mine[:, units]), dot_nt(d_pre, w1_other[:, units])
        part_mine, part_other = terms if k == 0 else (part_mine + terms[0], part_other + terms[1])
    part_mine, part_other = part_mine.astype(BF), part_other.astype(BF)

    def finish(own, other):
        for columns, part in ((own, part_mine), (other, part_other)):
            if last:
                kept, away = parts

                @pl.when(flags_ref[1] == 0)
                def _():
                    kept[:, columns], away[:, columns] = part[:128], part[128:]

                @pl.when(flags_ref[1] != 0)
                def _():
                    kept[:, columns], away[:, columns] = part[128:], part[:128]
            else:
                parts[0][:, columns] = part

    both_orders(finish)
    for part, out in zip(parts, part_outs):
        depart(part, out)
    for copy in departures:
        copy.wait()


def expert_rows(last, flags, earlier, got, weights, cost=SMALL):
    rows = 256 if last else 192
    parts = [(128, D)] * 2 if last else [(192, D)]
    outs = [(rows, D), (rows, 3 * D), *parts]
    anywhere = pl.BlockSpec(memory_space=pl.ANY)
    buffers = [(HALF, D)] * 2 + [(D, HALF)] * 2 + [got.shape] + [(rows, D)] * 4 + [(rows, 2 * D)] + parts
    return pl.pallas_call(
        functools.partial(expert_kernel, last),
        in_specs=[
            pl.BlockSpec(memory_space=pltpu.SMEM), *[anywhere] * 6
        ],
        out_specs=(anywhere,) * len(outs),
        out_shape=tuple(hbm_shape(shape) for shape in outs),
        scratch_shapes=[
            *(pltpu.VMEM(shape, BF) for shape in buffers),
            pltpu.SemaphoreType.DMA((9,)),
            pltpu.SemaphoreType.DMA((5,)),
        ],
        compiler_params=params(40),
        cost_estimate=cost,
        name="expert_last" if last else "expert_main",
    )(flags, in_hbm(earlier), got, *(in_hbm(weight) for weight in weights))


def weight_grads_kernel(*refs):
    in_ref, out_ref = refs[-2:]
    first = second = None
    for i in range(0, 24, 4):
        token_ref, grad_ref, hidden_ref, dpre_ref = refs[i:i + 4]
        a, b = dot_tn(token_ref[...], dpre_ref[...]), dot_tn(hidden_ref[...], grad_ref[...])
        first, second = (a, b) if first is None else (first + a, second + b)
    in_ref[...] = first.astype(BF)
    out_ref[...] = second.astype(BF)


def weight_grads(sets):
    specs, operands = [], []

    def take(x, block, moves):
        operands.append(in_hbm(x))
        index = (lambda h: (0, block + h)) if moves else (lambda h: (0, block))
        specs.append(pl.BlockSpec((x.shape[0], HALF), index))

    for mine, send, received in sets:
        for near, far in ((mine, send), (received, received)):
            take(near, 0, False)
            take(near, 1, False)
            take(far, 2, True)
            take(far, 4, True)
    return pl.pallas_call(
        weight_grads_kernel,
        grid=(2,),
        in_specs=specs,
        out_specs=(
            pl.BlockSpec((HALF, HALF), lambda h: (0, h)),
            pl.BlockSpec((HALF, HALF), lambda h: (h, 0)),
        ),
        out_shape=(hbm_shape((HALF, D)), hbm_shape((D, HALF))),
        compiler_params=params(48),
        cost_estimate=SMALL,
        name="weight_grads",
    )(*operands)


def merge_kernel(main_a, main_b, last_a, last_b, out_ref):
    row, column = iota((256, 128), 0), iota((256, 128), 1)
    target = ((column & 31) << 3) + (column >> 5)
    row6, column6 = iota((256, 192), 0), iota((256, 192), 1)
    spread = mask(row6 == ((column6 & 31) << 3) + (column6 >> 5))
    three = (main_a[...].astype(F32) + main_b[...].astype(F32)).astype(BF)
    two = (last_a[...].astype(F32) + last_b[...].astype(F32)).astype(BF)
    four = jnp.concatenate([three, two[:32]], axis=0)
    folded = dot(mask(row == target), four[:, :768]) + dot(mask(row == target + 4), four[:, 768:])
    out_ref[:, :768] = folded.astype(BF)
    fifth = jnp.concatenate([two[32:, j * 256:(j + 1) * 256] for j in range(6)], axis=0)
    out_ref[:, 768:] = dot(spread, fifth).astype(BF)


def merge(*parts):
    return pl.pallas_call(
        merge_kernel,
        grid=(2,),
        in_specs=[pl.BlockSpec((rows, D), lambda g: (g, 0)) for rows in (96, 96, 64, 64)],
        out_specs=pl.BlockSpec((256, 1024), lambda g: (g, 0)),
        out_shape=hbm_shape((512, 1024)),
        compiler_params=params(),
        cost_estimate=SMALL,
        name="merge",
    )(in_hbm(parts[0]), parts[1], in_hbm(parts[2]), parts[3])


def combine_kernel(routes_ref, got_ref, earlier_ref, out_ref):
    _, match, rank = slot_matches(routes_ref[...])
    inner = iota((EXPERTS * 8, TOK), 0) & 7
    chosen = match & (rank == (inner & 3).astype(F32))
    sides = [mask(chosen & (inner < 4)), mask(chosen & (inner >= 4))]
    chosen = match & (rank == 4.0)
    for j in range(6):
        columns = slice((j % 3) * 256, (j % 3 + 1) * 256)
        total = dot_tn(sides[j // 3], got_ref[:, columns])
        total += dot_tn(mask(chosen & (inner == j)), got_ref[:, 768:])
        out_ref[:, j * 256:(j + 1) * 256] = total.astype(BF)


def combine(routes_t, got, earlier):
    return pl.pallas_call(
        combine_kernel,
        in_specs=[whole(routes_t.shape), whole(got.shape), pl.BlockSpec(memory_space=pl.ANY)],
        out_specs=whole((TOK, D)),
        out_shape=jax.ShapeDtypeStruct((TOK, D), BF),
        compiler_params=params(),
        cost_estimate=SMALL,
        name="combine",
    )(routes_t, got, in_hbm(earlier))


def per_device(tokens, out_grad, routes, gate_probs, weight_in, weight_out):
    chips = [(i, i ^ 1) for i in range(128)]
    cores = [(0, 1), (1, 0)]
    outer = [4 * i + x for i in range(32) for x in (0, 3)]
    inner = [4 * i + x for i in range(32) for x in (1, 2)]
    halves, everyone = [outer, inner], [outer + inner]
    place = lax.axis_index("expert") & 3
    group = jnp.where((place == 1) | (place == 2), 1, 0)
    flags = jnp.stack([lax.axis_index("dp"), group]).astype(jnp.int32)

    def exchange(rows, groups):
        count = len(groups[0])
        chunked = rows.reshape(count, rows.shape[0] // count, rows.shape[1])
        got = lax.all_to_all(
            chunked, "expert", split_axis=0, concat_axis=0, tiled=True, axis_index_groups=groups
        )
        return got.reshape(rows.shape)

    def to_other_core(x):
        return lax.ppermute(x, "dp", cores)

    routes_t, gates_t = routes.T, gate_probs.T
    send_main = pack(False, routes_t, gates_t, tokens, out_grad)
    send_last = pack(True, routes_t, gates_t, tokens, out_grad)
    weight_sent = after(weight_out, send_last)
    weights = (weight_in, to_other_core(weight_in), weight_out, to_other_core(weight_sent))
    own_got = exchange(send_main, halves)
    pair_got = lax.ppermute(own_got, "expert", chips)
    own_mine, own_send, own_part = expert_rows(False, flags, send_main, own_got, weights)
    last_got = exchange(send_last, everyone)
    pair_mine, pair_send, pair_part = expert_rows(False, flags, own_part, pair_got, weights, LARGE)
    other_main = lax.ppermute(pair_part, "expert", chips)
    last_mine, last_send, last_part, last_away = expert_rows(True, flags, pair_part, last_got, weights)
    other_last = lax.ppermute(last_away, "expert", chips)
    merged = merge(own_part, other_main, last_part, other_last)
    got = exchange(merged, halves)
    grad_in, grad_out = weight_grads([
        (own_mine, own_send, to_other_core(own_send)),
        (pair_mine, pair_send, to_other_core(pair_send)),
        (after(last_mine, merged), last_send, to_other_core(last_send)),
    ])
    return combine(routes_t, got, grad_in), grad_in, grad_out


def solution(mesh):
    return jax.shard_map(
        per_device,
        mesh=mesh,
        in_specs=(
            P(("dp", "expert"), None),
            P(("dp", "expert"), None),
            P(("dp", "expert"), None),
            P(("dp", "expert"), None),
            P("dp", "expert"),
            P("expert", "dp"),
        ),
        out_specs=(P(("dp", "expert"), None), P("dp", "expert"), P("expert", "dp")),
        check_vma=False,
    )
```

```python
import functools

import jax
import jax.numpy as jnp
from jax import lax
from jax.experimental import pallas as pl
from jax.experimental.pallas import tpu as pltpu
from jax.sharding import PartitionSpec as P

ROOT_TWO_PI = 0.7978845608
CUBIC = 0.044715
BF = jnp.bfloat16
F32 = jnp.float32
D = 1536
TOK = 128
EXPERTS = 64
HALF = 768
LARGE = pl.CostEstimate(flops=10**11, bytes_accessed=10**8, transcendentals=0)
SMALL = pl.CostEstimate(flops=1, bytes_accessed=1, transcendentals=0)


def iota(shape, dim):
    return lax.broadcasted_iota(jnp.int32, shape, dim)


def mask(condition):
    return jnp.where(condition, 1.0, 0.0).astype(BF)


def dot(a, b):
    return jnp.dot(a, b, preferred_element_type=F32)


def dot_nt(a, b):
    return lax.dot_general(a, b, (((1,), (1,)), ((), ())), preferred_element_type=F32)


def dot_tn(a, b):
    return lax.dot_general(a, b, (((0,), (0,)), ((), ())), preferred_element_type=F32)


def whole(shape):
    return pl.BlockSpec(shape, lambda *_: (0,) * len(shape))


def params(mib=40):
    return pltpu.CompilerParams(vmem_limit_bytes=mib * 2**20)


def in_hbm(x):
    return pltpu.with_memory_space_constraint(x, pltpu.HBM)


def hbm_shape(shape):
    return pltpu.HBM(shape, BF)


def after_kernel(x_ref, earlier_ref, out_ref):
    pass


def after(x, earlier):
    anywhere = pl.BlockSpec(memory_space=pl.ANY)
    return pl.pallas_call(
        after_kernel,
        in_specs=[anywhere, anywhere],
        out_specs=anywhere,
        out_shape=jax.ShapeDtypeStruct(x.shape, x.dtype),
        input_output_aliases={0: 0},
        cost_estimate=SMALL,
        name="after",
    )(in_hbm(x), in_hbm(earlier))


def slot_matches(routes_t):
    expert = iota((EXPERTS * 8, TOK), 0) >> 3
    first = routes_t[0:1, :] == expert
    match = first | (routes_t[1:2, :] == expert)
    earlier = mask(iota((TOK, TOK), 0) < iota((TOK, TOK), 1))
    rank = dot(mask(match), earlier)
    return first, match, rank


def pack_main_kernel(routes_ref, gates_ref, tokens_ref, grads_ref, main_ref, rows_ref, sems):
    first, match, rank = slot_matches(routes_ref[...])
    gate = jnp.where(first, gates_ref[0:1, :], gates_ref[1:2, :])
    inner = iota((EXPERTS * 8, TOK), 0) & 7
    place = jnp.where(inner < 3, inner, inner - 3)
    chosen = match & (rank == place.astype(F32)) & (inner < 6)
    from_tokens, from_grads = mask(chosen & (inner < 3)), mask(chosen & (inner >= 3))
    copies = []
    token_tail, grad_tail = tokens_ref[:, 1152:], grads_ref[:, 1152:]
    for j in range(3):
        columns = slice(j * 384, (j + 1) * 384)
        tail = match & (rank == float(j)) & (inner >= 6)
        scale = jnp.sum(jnp.where(chosen | tail, gate, 0.0), axis=1, keepdims=True)
        rows = dot(
            jnp.concatenate([from_tokens, mask(tail & (inner == 6))], axis=1),
            jnp.concatenate([tokens_ref[:, columns], token_tail], axis=0),
        )
        rows += scale * dot(
            jnp.concatenate([from_grads, mask(tail & (inner == 7))], axis=1),
            jnp.concatenate([grads_ref[:, columns], grad_tail], axis=0),
        )
        rows_ref[j] = rows.astype(BF)
        copies.append(pltpu.make_async_copy(rows_ref.at[j], main_ref.at[:, pl.ds(j * 384, 384)], sems.at[j]))
        copies[j].start()
    for copy in copies:
        copy.wait()


def pack_last_kernel(routes_ref, gates_ref, tokens_ref, grads_ref, last_ref):
    first, match, rank = slot_matches(routes_ref[...])
    gate = jnp.where(first, gates_ref[0:1, :], gates_ref[1:2, :])
    inner = iota((EXPERTS * 8, TOK), 0) & 7
    quarter = inner & 3
    chosen = match & (rank == (3 + (quarter & 1)).astype(F32))
    scale = jnp.sum(jnp.where(chosen, gate, 0.0), axis=1, keepdims=True)
    rows = jnp.zeros((EXPERTS * 8, 768), F32)
    for j in range(2):
        side = chosen & ((inner >> 2) == j)
        columns = slice(j * 768, (j + 1) * 768)
        rows += dot(mask(side & (quarter < 2)), tokens_ref[:, columns])
        rows += dot(mask(side & (quarter >= 2)), grads_ref[:, columns]) * scale
    last = rows.astype(BF)
    last_ref[0:512, :] = last
    last_ref[512:1024, :] = last


def pack(last, *operands):
    shape = (1024, 768) if last else (512, 1152)
    scratch = [] if last else [pltpu.VMEM((3, 512, 384), BF), pltpu.SemaphoreType.DMA((3,))]
    return pl.pallas_call(
        pack_last_kernel if last else pack_main_kernel,
        out_specs=whole(shape) if last else pl.BlockSpec(memory_space=pl.ANY),
        out_shape=hbm_shape(shape),
        scratch_shapes=scratch,
        compiler_params=params(),
        cost_estimate=SMALL,
        name="pack_last" if last else "pack_main",
    )(*map(in_hbm, operands))


def unpack(last, got_ref, token_ref, grad_ref):
    row, column = iota((256, 256), 0), iota((256, 256), 1)
    move = mask(column == ((row & 31) << 3) + (row >> 5))
    for g in range(got_ref.shape[0] // 256):
        rows = dot(move, got_ref[g * 256:(g + 1) * 256, :]).astype(BF)
        if last:
            for j in range(2):
                columns = slice(j * 768, (j + 1) * 768)
                token_ref[g * 64:(g + 1) * 64, columns] = rows[j * 128:j * 128 + 64]
                grad_ref[g * 64:(g + 1) * 64, columns] = rows[j * 128 + 64:j * 128 + 128]
        else:
            token_ref[g * 96:(g + 1) * 96, :1152] = rows[:96]
            grad_ref[g * 96:(g + 1) * 96, :1152] = rows[96:192]
            for j in range(3):
                target = slice(g * 96 + j * 32, g * 96 + (j + 1) * 32)
                token_ref[target, 1152:] = rows[192:224, j * 384:(j + 1) * 384]
                grad_ref[target, 1152:] = rows[224:256, j * 384:(j + 1) * 384]


def expert_kernel(last, away, flags_ref, earlier_ref, got_ref, in_mine, in_other, out_mine, out_other, *rest):
    mine_out, send_out, part_out = rest[:3]
    w1_mine, w1_other, w2_mine, w2_other, got, token, grad, mine, send, units_out, part, loads, stores = rest[3:]
    low, high = pl.ds(0, HALF), pl.ds(HALF, HALF)
    first = flags_ref[0] == 0
    weights = ((in_mine, w1_mine), (in_other, w1_other), (out_mine, w2_mine), (out_other, w2_other))
    arrivals = []
    for source, target in weights:
        half = source.shape[0] // 2
        for k in range(2):
            rows = pl.ds(k * half, half)
            arrivals.append(pltpu.make_async_copy(source.at[rows, :], target.at[rows, :], loads.at[len(arrivals)]))
    if last:
        group = 1 - flags_ref[1] if away else flags_ref[1]
        got_ref = got_ref.at[pl.ds(pl.multiple_of(group * 512, 512), 512), :]
    got_here = pltpu.make_async_copy(got_ref, got, loads.at[8])
    got_here.start()
    for k in (0, 1, 2, 3, 4, 6, 5, 7):
        arrivals[k].start()
    got_here.wait()
    unpack(last, got, token, grad)

    def both_orders(run):
        pl.when(first)(lambda: run(low, high))
        pl.when(jnp.logical_not(first))(lambda: run(high, low))

    def split(own, other):
        mine[:, low] = token[:, own]
        mine[:, high] = grad[:, own]
        send[:, low] = token[:, other]
        send[:, high] = grad[:, other]

    both_orders(split)
    departures = []

    def depart(source, target):
        departures.append(pltpu.make_async_copy(source, target, stores.at[len(departures)]))
        departures[-1].start()

    pre = part_mine = part_other = None
    for k, (rows, w1) in enumerate(((mine, w1_mine), (mine, w1_mine), (send, w1_other), (send, w1_other))):
        arrivals[k].wait()
        chunk = pl.ds((k % 2) * (HALF // 2), HALF // 2)
        term = dot(rows[:, chunk], w1[chunk, :])
        pre = term if pre is None else pre + term
    for k in range(2):
        units = slice(k * HALF, (k + 1) * HALF)
        arrivals[4 + k].wait()
        arrivals[6 + k].wait()
        back = dot_nt(mine[:, high], w2_mine[units, :]) + dot_nt(send[:, high], w2_other[units, :])
        value = pre[:, units]
        square = value * value
        th = jnp.tanh(ROOT_TWO_PI * (value + CUBIC * square * value))
        half = 0.5 * (1.0 + th)
        slope = half + 0.5 * value * (1.0 - th * th) * ROOT_TWO_PI * (1.0 + 3.0 * CUBIC * square)
        d_pre = (back * slope).astype(BF)
        units_out[:, k * HALF:(k + 1) * HALF] = (value * half).astype(BF)
        units_out[:, (2 + k) * HALF:(3 + k) * HALF] = d_pre
        if k == 1:
            depart(mine, mine_out)
            depart(send, send_out.at[:, pl.ds(0, D)])
            depart(units_out, send_out.at[:, pl.ds(D, 2 * D)])
        terms = dot_nt(d_pre, w1_mine[:, units]), dot_nt(d_pre, w1_other[:, units])
        part_mine, part_other = terms if k == 0 else (part_mine + terms[0], part_other + terms[1])
    part_mine, part_other = part_mine.astype(BF), part_other.astype(BF)

    def finish(own, other):
        part[:, own] = part_mine
        part[:, other] = part_other

    both_orders(finish)
    depart(part, part_out)
    for copy in departures:
        copy.wait()


def expert_rows(last, flags, earlier, got, weights, cost=SMALL, away=False):
    rows = 128 if last else 192
    outs = [(rows, D), (rows, 3 * D), (rows, D)]
    anywhere = pl.BlockSpec(memory_space=pl.ANY)
    buffers = [(HALF, D)] * 2 + [(D, HALF)] * 2 + [(512, got.shape[1])] + [(rows, D)] * 4 + [(rows, 2 * D), (rows, D)]
    return pl.pallas_call(
        functools.partial(expert_kernel, last, away),
        in_specs=[
            pl.BlockSpec(memory_space=pltpu.SMEM), *[anywhere] * 6
        ],
        out_specs=(anywhere,) * len(outs),
        out_shape=tuple(hbm_shape(shape) for shape in outs),
        scratch_shapes=[
            *(pltpu.VMEM(shape, BF) for shape in buffers),
            pltpu.SemaphoreType.DMA((9,)),
            pltpu.SemaphoreType.DMA((4,)),
        ],
        compiler_params=params(40),
        cost_estimate=cost,
        name="expert_last" if last else "expert_main",
    )(flags, in_hbm(earlier), got, *(in_hbm(weight) for weight in weights))


def weight_grads_kernel(*refs):
    in_ref, out_ref = refs[-2:]
    first = second = None
    for i in range(0, len(refs) - 2, 4):
        token_ref, grad_ref, hidden_ref, dpre_ref = refs[i:i + 4]
        a, b = dot_tn(token_ref[...], dpre_ref[...]), dot_tn(hidden_ref[...], grad_ref[...])
        first, second = (a, b) if first is None else (first + a, second + b)
    in_ref[...] = first.astype(BF)
    out_ref[...] = second.astype(BF)


def weight_grads(sets):
    specs, operands = [], []

    def take(x, block, moves):
        operands.append(in_hbm(x))
        index = (lambda h: (0, block + h)) if moves else (lambda h: (0, block))
        specs.append(pl.BlockSpec((x.shape[0], HALF), index))

    for mine, send, received in sets:
        for near, far in ((mine, send), (received, received)):
            take(near, 0, False)
            take(near, 1, False)
            take(far, 2, True)
            take(far, 4, True)
    return pl.pallas_call(
        weight_grads_kernel,
        grid=(2,),
        in_specs=specs,
        out_specs=(
            pl.BlockSpec((HALF, HALF), lambda h: (0, h)),
            pl.BlockSpec((HALF, HALF), lambda h: (h, 0)),
        ),
        out_shape=(hbm_shape((HALF, D)), hbm_shape((D, HALF))),
        compiler_params=params(48),
        cost_estimate=SMALL,
        name="weight_grads",
    )(*operands)


def merge_kernel(main_a, main_b, last_a, last_b, out_ref):
    row, column = iota((256, 128), 0), iota((256, 128), 1)
    target = ((column & 31) << 3) + (column >> 5)
    row6, column6 = iota((256, 192), 0), iota((256, 192), 1)
    spread = mask(row6 == ((column6 & 31) << 3) + (column6 >> 5))
    three = (main_a[...].astype(F32) + main_b[...].astype(F32)).astype(BF)
    two = (last_a[...].astype(F32) + last_b[...].astype(F32)).astype(BF)
    four = jnp.concatenate([three, two[:32]], axis=0)
    folded = dot(mask(row == target), four[:, :768]) + dot(mask(row == target + 4), four[:, 768:])
    out_ref[:, :768] = folded.astype(BF)
    fifth = jnp.concatenate([two[32:, j * 256:(j + 1) * 256] for j in range(6)], axis=0)
    out_ref[:, 768:] = dot(spread, fifth).astype(BF)


def merge(*parts):
    return pl.pallas_call(
        merge_kernel,
        grid=(2,),
        in_specs=[pl.BlockSpec((rows, D), lambda g: (g, 0)) for rows in (96, 96, 64, 64)],
        out_specs=pl.BlockSpec((256, 1024), lambda g: (g, 0)),
        out_shape=hbm_shape((512, 1024)),
        compiler_params=params(),
        cost_estimate=SMALL,
        name="merge",
    )(in_hbm(parts[0]), parts[1], in_hbm(parts[2]), parts[3])


def combine_kernel(routes_ref, got_ref, earlier_ref, out_ref):
    _, match, rank = slot_matches(routes_ref[...])
    inner = iota((EXPERTS * 8, TOK), 0) & 7
    chosen = match & (rank == (inner & 3).astype(F32))
    sides = [mask(chosen & (inner < 4)), mask(chosen & (inner >= 4))]
    chosen = match & (rank == 4.0)
    for j in range(6):
        columns = slice((j % 3) * 256, (j % 3 + 1) * 256)
        total = dot_tn(sides[j // 3], got_ref[:, columns])
        total += dot_tn(mask(chosen & (inner == j)), got_ref[:, 768:])
        out_ref[:, j * 256:(j + 1) * 256] = total.astype(BF)


def combine(routes_t, got, earlier):
    return pl.pallas_call(
        combine_kernel,
        in_specs=[whole(routes_t.shape), whole(got.shape), pl.BlockSpec(memory_space=pl.ANY)],
        out_specs=whole((TOK, D)),
        out_shape=jax.ShapeDtypeStruct((TOK, D), BF),
        compiler_params=params(),
        cost_estimate=SMALL,
        name="combine",
    )(routes_t, got, in_hbm(earlier))


def per_device(tokens, out_grad, routes, gate_probs, weight_in, weight_out):
    chips = [(i, i ^ 1) for i in range(128)]
    cores = [(0, 1), (1, 0)]
    outer = [4 * i + x for i in range(32) for x in (0, 3)]
    inner = [4 * i + x for i in range(32) for x in (1, 2)]
    halves, everyone = [outer, inner], [outer + inner]
    place = lax.axis_index("expert") & 3
    group = jnp.where((place == 1) | (place == 2), 1, 0)
    flags = jnp.stack([lax.axis_index("dp"), group]).astype(jnp.int32)

    def exchange(rows, groups):
        count = len(groups[0])
        chunked = rows.reshape(count, rows.shape[0] // count, rows.shape[1])
        got = lax.all_to_all(
            chunked, "expert", split_axis=0, concat_axis=0, tiled=True, axis_index_groups=groups
        )
        return got.reshape(rows.shape)

    def to_other_core(x):
        return lax.ppermute(x, "dp", cores)

    routes_t, gates_t = routes.T, gate_probs.T
    send_main = pack(False, routes_t, gates_t, tokens, out_grad)
    send_last = pack(True, routes_t, gates_t, tokens, out_grad)
    weight_sent = after(weight_out, send_last)
    weights = (weight_in, to_other_core(weight_in), weight_out, to_other_core(weight_sent))
    own_got = exchange(send_main, halves)
    pair_got = lax.ppermute(own_got, "expert", chips)
    own_mine, own_send, own_part = expert_rows(False, flags, send_main, own_got, weights)
    last_got = exchange(send_last, everyone)
    pair_mine, pair_send, pair_part = expert_rows(False, flags, own_part, pair_got, weights, LARGE)
    other_main = lax.ppermute(pair_part, "expert", chips)
    away_mine, away_send, away_part = expert_rows(True, flags, pair_part, last_got, weights, away=True)
    other_last = lax.ppermute(away_part, "expert", chips)
    last_mine, last_send, last_part = expert_rows(True, flags, away_part, last_got, weights)
    merged = merge(own_part, other_main, last_part, other_last)
    got = exchange(merged, halves)
    grad_in, grad_out = weight_grads([
        (own_mine, own_send, to_other_core(own_send)),
        (pair_mine, pair_send, to_other_core(pair_send)),
        (away_mine, away_send, to_other_core(away_send)),
        (after(last_mine, merged), last_send, to_other_core(last_send)),
    ])
    return combine(routes_t, got, grad_in), grad_in, grad_out


def solution(mesh):
    return jax.shard_map(
        per_device,
        mesh=mesh,
        in_specs=(
            P(("dp", "expert"), None),
            P(("dp", "expert"), None),
            P(("dp", "expert"), None),
            P(("dp", "expert"), None),
            P("dp", "expert"),
            P("expert", "dp"),
        ),
        out_specs=(P(("dp", "expert"), None), P("dp", "expert"), P("expert", "dp")),
        check_vma=False,
    )
```

```python
import functools

import jax
import jax.numpy as jnp
from jax import lax
from jax.experimental import pallas as pl
from jax.experimental.pallas import tpu as pltpu
from jax.sharding import PartitionSpec as P

ROOT_TWO_PI = 0.7978845608
CUBIC = 0.044715
BF = jnp.bfloat16
F32 = jnp.float32
D = 1536
TOK = 128
EXPERTS = 64
HALF = 768
LARGE = pl.CostEstimate(flops=10**11, bytes_accessed=10**8, transcendentals=0)
SMALL = pl.CostEstimate(flops=1, bytes_accessed=1, transcendentals=0)


def iota(shape, dim):
    return lax.broadcasted_iota(jnp.int32, shape, dim)


def mask(condition):
    return jnp.where(condition, 1.0, 0.0).astype(BF)


def dot(a, b):
    return jnp.dot(a, b, preferred_element_type=F32)


def dot_nt(a, b):
    return lax.dot_general(a, b, (((1,), (1,)), ((), ())), preferred_element_type=F32)


def dot_tn(a, b):
    return lax.dot_general(a, b, (((0,), (0,)), ((), ())), preferred_element_type=F32)


def whole(shape):
    return pl.BlockSpec(shape, lambda *_: (0,) * len(shape))


def params(mib=40):
    return pltpu.CompilerParams(vmem_limit_bytes=mib * 2**20)


def in_hbm(x):
    return pltpu.with_memory_space_constraint(x, pltpu.HBM)


def hbm_shape(shape):
    return pltpu.HBM(shape, BF)


def after_kernel(x_ref, earlier_ref, out_ref):
    pass


def after(x, earlier):
    anywhere = pl.BlockSpec(memory_space=pl.ANY)
    return pl.pallas_call(
        after_kernel,
        in_specs=[anywhere, anywhere],
        out_specs=anywhere,
        out_shape=jax.ShapeDtypeStruct(x.shape, x.dtype),
        input_output_aliases={0: 0},
        cost_estimate=SMALL,
        name="after",
    )(in_hbm(x), in_hbm(earlier))


def slot_matches(routes_t):
    expert = iota((EXPERTS * 8, TOK), 0) >> 3
    first = routes_t[0:1, :] == expert
    match = first | (routes_t[1:2, :] == expert)
    earlier = mask(iota((TOK, TOK), 0) < iota((TOK, TOK), 1))
    rank = dot(mask(match), earlier)
    return first, match, rank


def pack_main_kernel(routes_ref, gates_ref, tokens_ref, grads_ref, main_ref, rows_ref, sems):
    first, match, rank = slot_matches(routes_ref[...])
    gate = jnp.where(first, gates_ref[0:1, :], gates_ref[1:2, :])
    inner = iota((EXPERTS * 8, TOK), 0) & 7
    place = jnp.where(inner < 3, inner, inner - 3)
    chosen = match & (rank == place.astype(F32)) & (inner < 6)
    from_tokens, from_grads = mask(chosen & (inner < 3)), mask(chosen & (inner >= 3))
    copies = []
    token_tail, grad_tail = tokens_ref[:, 1152:], grads_ref[:, 1152:]
    for j in range(3):
        columns = slice(j * 384, (j + 1) * 384)
        tail = match & (rank == float(j)) & (inner >= 6)
        scale = jnp.sum(jnp.where(chosen | tail, gate, 0.0), axis=1, keepdims=True)
        rows = dot(
            jnp.concatenate([from_tokens, mask(tail & (inner == 6))], axis=1),
            jnp.concatenate([tokens_ref[:, columns], token_tail], axis=0),
        )
        rows += scale * dot(
            jnp.concatenate([from_grads, mask(tail & (inner == 7))], axis=1),
            jnp.concatenate([grads_ref[:, columns], grad_tail], axis=0),
        )
        rows_ref[j] = rows.astype(BF)
        copies.append(pltpu.make_async_copy(rows_ref.at[j], main_ref.at[:, pl.ds(j * 384, 384)], sems.at[j]))
        copies[j].start()
    for copy in copies:
        copy.wait()


def pack_last_kernel(routes_ref, gates_ref, tokens_ref, grads_ref, last_ref):
    first, match, rank = slot_matches(routes_ref[...])
    gate = jnp.where(first, gates_ref[0:1, :], gates_ref[1:2, :])
    inner = iota((EXPERTS * 8, TOK), 0) & 7
    quarter = inner & 3
    chosen = match & (rank == (3 + (quarter & 1)).astype(F32))
    scale = jnp.sum(jnp.where(chosen, gate, 0.0), axis=1, keepdims=True)
    rows = jnp.zeros((EXPERTS * 8, 768), F32)
    for j in range(2):
        side = chosen & ((inner >> 2) == j)
        columns = slice(j * 768, (j + 1) * 768)
        rows += dot(mask(side & (quarter < 2)), tokens_ref[:, columns])
        rows += dot(mask(side & (quarter >= 2)), grads_ref[:, columns]) * scale
    last = rows.astype(BF)
    last_ref[0:512, :] = last
    last_ref[512:1024, :] = last


def pack(last, *operands):
    shape = (1024, 768) if last else (512, 1152)
    scratch = [] if last else [pltpu.VMEM((3, 512, 384), BF), pltpu.SemaphoreType.DMA((3,))]
    return pl.pallas_call(
        pack_last_kernel if last else pack_main_kernel,
        out_specs=whole(shape) if last else pl.BlockSpec(memory_space=pl.ANY),
        out_shape=hbm_shape(shape),
        scratch_shapes=scratch,
        compiler_params=params(),
        cost_estimate=SMALL,
        name="pack_last" if last else "pack_main",
    )(*map(in_hbm, operands))


def unpack(last, got_ref, token_ref, grad_ref):
    row, column = iota((256, 256), 0), iota((256, 256), 1)
    move = mask(column == ((row & 31) << 3) + (row >> 5))
    for g in range(got_ref.shape[0] // 256):
        rows = dot(move, got_ref[g * 256:(g + 1) * 256, :]).astype(BF)
        if last:
            for j in range(2):
                columns = slice(j * 768, (j + 1) * 768)
                token_ref[g * 64:(g + 1) * 64, columns] = rows[j * 128:j * 128 + 64]
                grad_ref[g * 64:(g + 1) * 64, columns] = rows[j * 128 + 64:j * 128 + 128]
        else:
            token_ref[g * 96:(g + 1) * 96, :1152] = rows[:96]
            grad_ref[g * 96:(g + 1) * 96, :1152] = rows[96:192]
            for j in range(3):
                target = slice(g * 96 + j * 32, g * 96 + (j + 1) * 32)
                token_ref[target, 1152:] = rows[192:224, j * 384:(j + 1) * 384]
                grad_ref[target, 1152:] = rows[224:256, j * 384:(j + 1) * 384]


def expert_kernel(last, away, flags_ref, earlier_ref, got_ref, in_mine, in_other, out_mine, out_other, *rest):
    mine_out, send_out, part_out = rest[:3]
    w1_mine, w1_other, w2_mine, w2_other, got, token, grad, mine, send, units_out, part, loads, stores = rest[3:]
    low, high = pl.ds(0, HALF), pl.ds(HALF, HALF)
    first = flags_ref[0] == 0
    weights = ((in_mine, w1_mine), (in_other, w1_other), (out_mine, w2_mine), (out_other, w2_other))
    arrivals = []
    for source, target in weights:
        half = source.shape[0] // 2
        for k in range(2):
            rows = pl.ds(k * half, half)
            arrivals.append(pltpu.make_async_copy(source.at[rows, :], target.at[rows, :], loads.at[len(arrivals)]))
    if last:
        group = 1 - flags_ref[1] if away else flags_ref[1]
        got_ref = got_ref.at[pl.ds(pl.multiple_of(group * 512, 512), 512), :]
    got_here = pltpu.make_async_copy(got_ref, got, loads.at[8])
    got_here.start()
    for k in (0, 1, 2, 3, 4, 6, 5, 7):
        arrivals[k].start()
    got_here.wait()
    unpack(last, got, token, grad)

    def both_orders(run):
        pl.when(first)(lambda: run(low, high))
        pl.when(jnp.logical_not(first))(lambda: run(high, low))

    def split(own, other):
        mine[:, low] = token[:, own]
        mine[:, high] = grad[:, own]
        send[:, low] = token[:, other]
        send[:, high] = grad[:, other]

    both_orders(split)
    departures = []

    def depart(source, target):
        departures.append(pltpu.make_async_copy(source, target, stores.at[len(departures)]))
        departures[-1].start()

    pre = part_mine = part_other = None
    for k, (rows, w1) in enumerate(((mine, w1_mine), (mine, w1_mine), (send, w1_other), (send, w1_other))):
        arrivals[k].wait()
        chunk = pl.ds((k % 2) * (HALF // 2), HALF // 2)
        term = dot(rows[:, chunk], w1[chunk, :])
        pre = term if pre is None else pre + term
    for k in range(2):
        units = slice(k * HALF, (k + 1) * HALF)
        arrivals[4 + k].wait()
        arrivals[6 + k].wait()
        back = dot_nt(mine[:, high], w2_mine[units, :]) + dot_nt(send[:, high], w2_other[units, :])
        value = pre[:, units]
        square = value * value
        th = jnp.tanh(ROOT_TWO_PI * (value + CUBIC * square * value))
        half = 0.5 * (1.0 + th)
        slope = half + 0.5 * value * (1.0 - th * th) * ROOT_TWO_PI * (1.0 + 3.0 * CUBIC * square)
        d_pre = (back * slope).astype(BF)
        units_out[:, k * HALF:(k + 1) * HALF] = (value * half).astype(BF)
        units_out[:, (2 + k) * HALF:(3 + k) * HALF] = d_pre
        if k == 1:
            depart(mine, mine_out)
            depart(send, send_out.at[:, pl.ds(0, D)])
            depart(units_out, send_out.at[:, pl.ds(D, 2 * D)])
        terms = dot_nt(d_pre, w1_mine[:, units]), dot_nt(d_pre, w1_other[:, units])
        part_mine, part_other = terms if k == 0 else (part_mine + terms[0], part_other + terms[1])
    part_mine, part_other = part_mine.astype(BF), part_other.astype(BF)

    def finish(own, other):
        part[:, own] = part_mine
        part[:, other] = part_other

    both_orders(finish)
    depart(part, part_out)
    for copy in departures:
        copy.wait()


def expert_rows(last, flags, earlier, got, weights, cost=SMALL, away=False):
    rows = 128 if last else 192
    outs = [(rows, D), (rows, 3 * D), (rows, D)]
    anywhere = pl.BlockSpec(memory_space=pl.ANY)
    buffers = [(HALF, D)] * 2 + [(D, HALF)] * 2 + [(512, got.shape[1])] + [(rows, D)] * 4 + [(rows, 2 * D), (rows, D)]
    return pl.pallas_call(
        functools.partial(expert_kernel, last, away),
        in_specs=[
            pl.BlockSpec(memory_space=pltpu.SMEM), *[anywhere] * 6
        ],
        out_specs=(anywhere,) * len(outs),
        out_shape=tuple(hbm_shape(shape) for shape in outs),
        scratch_shapes=[
            *(pltpu.VMEM(shape, BF) for shape in buffers),
            pltpu.SemaphoreType.DMA((9,)),
            pltpu.SemaphoreType.DMA((4,)),
        ],
        compiler_params=params(40),
        cost_estimate=cost,
        name="expert_last" if last else "expert_main",
    )(flags, in_hbm(earlier), got, *(in_hbm(weight) for weight in weights))


def weight_grads_kernel(*refs):
    *operands, in_ref, out_ref = refs
    tokens, grads, hidden, d_pre = (
        jnp.concatenate([ref[...] for ref in operands[i::4]], axis=0) for i in range(4)
    )
    in_ref[...] = dot_tn(tokens, d_pre).astype(BF)
    out_ref[...] = dot_tn(hidden, grads).astype(BF)


def weight_grads(sets):
    specs, operands = [], []

    def take(x, block, moves):
        operands.append(in_hbm(x))
        index = (lambda h: (0, block + h)) if moves else (lambda h: (0, block))
        specs.append(pl.BlockSpec((x.shape[0], HALF), index))

    for mine, send, received in sets:
        for near, far in ((mine, send), (received, received)):
            take(near, 0, False)
            take(near, 1, False)
            take(far, 2, True)
            take(far, 4, True)
    return pl.pallas_call(
        weight_grads_kernel,
        grid=(2,),
        in_specs=specs,
        out_specs=(
            pl.BlockSpec((HALF, HALF), lambda h: (0, h)),
            pl.BlockSpec((HALF, HALF), lambda h: (h, 0)),
        ),
        out_shape=(hbm_shape((HALF, D)), hbm_shape((D, HALF))),
        compiler_params=params(48),
        cost_estimate=SMALL,
        name="weight_grads",
    )(*operands)


def merge_kernel(main_a, main_b, last_a, last_b, out_ref):
    row, column = iota((256, 128), 0), iota((256, 128), 1)
    target = ((column & 31) << 3) + (column >> 5)
    row6, column6 = iota((256, 192), 0), iota((256, 192), 1)
    spread = mask(row6 == ((column6 & 31) << 3) + (column6 >> 5))
    three = (main_a[...].astype(F32) + main_b[...].astype(F32)).astype(BF)
    two = (last_a[...].astype(F32) + last_b[...].astype(F32)).astype(BF)
    four = jnp.concatenate([three, two[:32]], axis=0)
    folded = dot(mask(row == target), four[:, :768]) + dot(mask(row == target + 4), four[:, 768:])
    out_ref[:, :768] = folded.astype(BF)
    fifth = jnp.concatenate([two[32:, j * 256:(j + 1) * 256] for j in range(6)], axis=0)
    out_ref[:, 768:] = dot(spread, fifth).astype(BF)


def merge(*parts):
    return pl.pallas_call(
        merge_kernel,
        grid=(2,),
        in_specs=[pl.BlockSpec((rows, D), lambda g: (g, 0)) for rows in (96, 96, 64, 64)],
        out_specs=pl.BlockSpec((256, 1024), lambda g: (g, 0)),
        out_shape=hbm_shape((512, 1024)),
        compiler_params=params(),
        cost_estimate=SMALL,
        name="merge",
    )(in_hbm(parts[0]), parts[1], in_hbm(parts[2]), parts[3])


def combine_kernel(routes_ref, got_ref, earlier_ref, out_ref):
    _, match, rank = slot_matches(routes_ref[...])
    inner = iota((EXPERTS * 8, TOK), 0) & 7
    chosen = match & (rank == (inner & 3).astype(F32))
    sides = [mask(chosen & (inner < 4)), mask(chosen & (inner >= 4))]
    chosen = match & (rank == 4.0)
    for j in range(6):
        columns = slice((j % 3) * 256, (j % 3 + 1) * 256)
        total = dot_tn(sides[j // 3], got_ref[:, columns])
        total += dot_tn(mask(chosen & (inner == j)), got_ref[:, 768:])
        out_ref[:, j * 256:(j + 1) * 256] = total.astype(BF)


def combine(routes_t, got, earlier):
    return pl.pallas_call(
        combine_kernel,
        in_specs=[whole(routes_t.shape), whole(got.shape), pl.BlockSpec(memory_space=pl.ANY)],
        out_specs=whole((TOK, D)),
        out_shape=jax.ShapeDtypeStruct((TOK, D), BF),
        compiler_params=params(),
        cost_estimate=SMALL,
        name="combine",
    )(routes_t, got, in_hbm(earlier))


def per_device(tokens, out_grad, routes, gate_probs, weight_in, weight_out):
    chips = [(i, i ^ 1) for i in range(128)]
    cores = [(0, 1), (1, 0)]
    outer = [4 * i + x for i in range(32) for x in (0, 3)]
    inner = [4 * i + x for i in range(32) for x in (1, 2)]
    halves, everyone = [outer, inner], [outer + inner]
    place = lax.axis_index("expert") & 3
    group = jnp.where((place == 1) | (place == 2), 1, 0)
    flags = jnp.stack([lax.axis_index("dp"), group]).astype(jnp.int32)

    def exchange(rows, groups):
        count = len(groups[0])
        chunked = rows.reshape(count, rows.shape[0] // count, rows.shape[1])
        got = lax.all_to_all(
            chunked, "expert", split_axis=0, concat_axis=0, tiled=True, axis_index_groups=groups
        )
        return got.reshape(rows.shape)

    def to_other_core(x):
        return lax.ppermute(x, "dp", cores)

    routes_t, gates_t = routes.T, gate_probs.T
    send_main = pack(False, routes_t, gates_t, tokens, out_grad)
    send_last = pack(True, routes_t, gates_t, tokens, out_grad)
    weight_sent = after(weight_out, send_last)
    weights = (weight_in, to_other_core(weight_in), weight_out, to_other_core(weight_sent))
    own_got = exchange(send_main, halves)
    pair_got = lax.ppermute(own_got, "expert", chips)
    own_mine, own_send, own_part = expert_rows(False, flags, send_main, own_got, weights)
    last_got = exchange(send_last, everyone)
    pair_mine, pair_send, pair_part = expert_rows(False, flags, own_part, pair_got, weights, LARGE)
    other_main = lax.ppermute(pair_part, "expert", chips)
    away_mine, away_send, away_part = expert_rows(True, flags, pair_part, last_got, weights, away=True)
    other_last = lax.ppermute(away_part, "expert", chips)
    last_mine, last_send, last_part = expert_rows(True, flags, away_part, last_got, weights)
    merged = merge(own_part, other_main, last_part, other_last)
    got = exchange(merged, halves)
    grad_in, grad_out = weight_grads([
        (own_mine, own_send, to_other_core(own_send)),
        (pair_mine, pair_send, to_other_core(pair_send)),
        (away_mine, away_send, to_other_core(away_send)),
        (after(last_mine, merged), last_send, to_other_core(last_send)),
    ])
    return combine(routes_t, got, grad_in), grad_in, grad_out


def solution(mesh):
    return jax.shard_map(
        per_device,
        mesh=mesh,
        in_specs=(
            P(("dp", "expert"), None),
            P(("dp", "expert"), None),
            P(("dp", "expert"), None),
            P(("dp", "expert"), None),
            P("dp", "expert"),
            P("expert", "dp"),
        ),
        out_specs=(P(("dp", "expert"), None), P("dp", "expert"), P("expert", "dp")),
        check_vma=False,
    )
```

```python
import functools

import jax
import jax.numpy as jnp
from jax import lax
from jax.experimental import pallas as pl
from jax.experimental.pallas import tpu as pltpu
from jax.sharding import PartitionSpec as P

ROOT_TWO_PI = 0.7978845608
CUBIC = 0.044715
BF = jnp.bfloat16
F32 = jnp.float32
D = 1536
TOK = 128
EXPERTS = 64
HALF = 768
LARGE = pl.CostEstimate(flops=10**11, bytes_accessed=10**8, transcendentals=0)
SMALL = pl.CostEstimate(flops=1, bytes_accessed=1, transcendentals=0)


def iota(shape, dim):
    return lax.broadcasted_iota(jnp.int32, shape, dim)


def mask(condition):
    return jnp.where(condition, 1.0, 0.0).astype(BF)


def dot(a, b):
    return jnp.dot(a, b, preferred_element_type=F32)


def dot_nt(a, b):
    return lax.dot_general(a, b, (((1,), (1,)), ((), ())), preferred_element_type=F32)


def dot_tn(a, b):
    return lax.dot_general(a, b, (((0,), (0,)), ((), ())), preferred_element_type=F32)


def whole(shape):
    return pl.BlockSpec(shape, lambda *_: (0,) * len(shape))


def params(mib=40):
    return pltpu.CompilerParams(vmem_limit_bytes=mib * 2**20)


def in_hbm(x):
    return pltpu.with_memory_space_constraint(x, pltpu.HBM)


def hbm_shape(shape):
    return pltpu.HBM(shape, BF)


def after_kernel(x_ref, earlier_ref, out_ref):
    pass


def after(x, earlier):
    anywhere = pl.BlockSpec(memory_space=pl.ANY)
    return pl.pallas_call(
        after_kernel,
        in_specs=[anywhere, anywhere],
        out_specs=anywhere,
        out_shape=jax.ShapeDtypeStruct(x.shape, x.dtype),
        input_output_aliases={0: 0},
        cost_estimate=SMALL,
        name="after",
    )(in_hbm(x), in_hbm(earlier))


def slot_matches(routes_t):
    expert = iota((EXPERTS * 8, TOK), 0) >> 3
    first = routes_t[0:1, :] == expert
    match = first | (routes_t[1:2, :] == expert)
    earlier = mask(iota((TOK, TOK), 0) < iota((TOK, TOK), 1))
    rank = dot(mask(match), earlier)
    return first, match, rank


def pack_main_kernel(routes_ref, gates_ref, tokens_ref, grads_ref, main_ref, rows_ref, sems):
    first, match, rank = slot_matches(routes_ref[...])
    gate = jnp.where(first, gates_ref[0:1, :], gates_ref[1:2, :])
    inner = iota((EXPERTS * 8, TOK), 0) & 7
    place = jnp.where(inner < 3, inner, inner - 3)
    chosen = match & (rank == place.astype(F32)) & (inner < 6)
    from_tokens, from_grads = mask(chosen & (inner < 3)), mask(chosen & (inner >= 3))
    copies = []
    token_tail, grad_tail = tokens_ref[:, 1152:], grads_ref[:, 1152:]
    for j in range(3):
        columns = slice(j * 384, (j + 1) * 384)
        tail = match & (rank == float(j)) & (inner >= 6)
        scale = jnp.sum(jnp.where(chosen | tail, gate, 0.0), axis=1, keepdims=True)
        rows = dot(
            jnp.concatenate([from_tokens, mask(tail & (inner == 6))], axis=1),
            jnp.concatenate([tokens_ref[:, columns], token_tail], axis=0),
        )
        rows += scale * dot(
            jnp.concatenate([from_grads, mask(tail & (inner == 7))], axis=1),
            jnp.concatenate([grads_ref[:, columns], grad_tail], axis=0),
        )
        rows_ref[j] = rows.astype(BF)
        copies.append(pltpu.make_async_copy(rows_ref.at[j], main_ref.at[:, pl.ds(j * 384, 384)], sems.at[j]))
        copies[j].start()
    for copy in copies:
        copy.wait()


def pack_last_kernel(routes_ref, gates_ref, tokens_ref, grads_ref, last_ref):
    first, match, rank = slot_matches(routes_ref[...])
    gate = jnp.where(first, gates_ref[0:1, :], gates_ref[1:2, :])
    inner = iota((EXPERTS * 8, TOK), 0) & 7
    quarter = inner & 3
    chosen = match & (rank == (3 + (quarter & 1)).astype(F32))
    scale = jnp.sum(jnp.where(chosen, gate, 0.0), axis=1, keepdims=True)
    rows = jnp.zeros((EXPERTS * 8, 768), F32)
    for j in range(2):
        side = chosen & ((inner >> 2) == j)
        columns = slice(j * 768, (j + 1) * 768)
        rows += dot(mask(side & (quarter < 2)), tokens_ref[:, columns])
        rows += dot(mask(side & (quarter >= 2)), grads_ref[:, columns]) * scale
    last = rows.astype(BF)
    last_ref[0:512, :] = last
    last_ref[512:1024, :] = last


def pack(last, *operands):
    shape = (1024, 768) if last else (512, 1152)
    scratch = [] if last else [pltpu.VMEM((3, 512, 384), BF), pltpu.SemaphoreType.DMA((3,))]
    return pl.pallas_call(
        pack_last_kernel if last else pack_main_kernel,
        out_specs=whole(shape) if last else pl.BlockSpec(memory_space=pl.ANY),
        out_shape=hbm_shape(shape),
        scratch_shapes=scratch,
        compiler_params=params(),
        cost_estimate=SMALL,
        name="pack_last" if last else "pack_main",
    )(*map(in_hbm, operands))


def unpack(last, got_ref, token_ref, grad_ref):
    row, column = iota((256, 256), 0), iota((256, 256), 1)
    move = mask(column == ((row & 31) << 3) + (row >> 5))
    for g in range(got_ref.shape[0] // 256):
        rows = dot(move, got_ref[g * 256:(g + 1) * 256, :]).astype(BF)
        if last:
            for j in range(2):
                columns = slice(j * 768, (j + 1) * 768)
                token_ref[g * 64:(g + 1) * 64, columns] = rows[j * 128:j * 128 + 64]
                grad_ref[g * 64:(g + 1) * 64, columns] = rows[j * 128 + 64:j * 128 + 128]
        else:
            token_ref[g * 96:(g + 1) * 96, :1152] = rows[:96]
            grad_ref[g * 96:(g + 1) * 96, :1152] = rows[96:192]
            for j in range(3):
                target = slice(g * 96 + j * 32, g * 96 + (j + 1) * 32)
                token_ref[target, 1152:] = rows[192:224, j * 384:(j + 1) * 384]
                grad_ref[target, 1152:] = rows[224:256, j * 384:(j + 1) * 384]


def expert_kernel(last, flags_ref, earlier_ref, got_ref, in_mine, in_other, out_mine, out_other, *rest):
    count = 4 if last else 3
    mine_out, send_out, *part_outs = rest[:count]
    w1_mine, w1_other, w2_mine, w2_other, got, token, grad, mine, send, units_out, *parts, loads, stores = rest[count:]
    low, high = pl.ds(0, HALF), pl.ds(HALF, HALF)
    first = flags_ref[0] == 0
    weights = ((in_mine, w1_mine), (in_other, w1_other), (out_mine, w2_mine), (out_other, w2_other))
    arrivals = []
    for source, target in weights:
        half = source.shape[0] // 2
        for k in range(2):
            rows = pl.ds(k * half, half)
            arrivals.append(pltpu.make_async_copy(source.at[rows, :], target.at[rows, :], loads.at[len(arrivals)]))
    got_here = pltpu.make_async_copy(got_ref, got, loads.at[8])
    got_here.start()
    for k in (0, 1, 2, 3, 4, 6, 5, 7):
        arrivals[k].start()
    got_here.wait()
    unpack(last, got, token, grad)

    def both_orders(run):
        pl.when(first)(lambda: run(low, high))
        pl.when(jnp.logical_not(first))(lambda: run(high, low))

    def split(own, other):
        mine[:, low] = token[:, own]
        mine[:, high] = grad[:, own]
        send[:, low] = token[:, other]
        send[:, high] = grad[:, other]

    both_orders(split)
    departures = []

    def depart(source, target):
        departures.append(pltpu.make_async_copy(source, target, stores.at[len(departures)]))
        departures[-1].start()

    pre = part_mine = part_other = None
    for k, (rows, w1) in enumerate(((mine, w1_mine), (mine, w1_mine), (send, w1_other), (send, w1_other))):
        arrivals[k].wait()
        part = pl.ds((k % 2) * (HALF // 2), HALF // 2)
        term = dot(rows[:, part], w1[part, :])
        pre = term if pre is None else pre + term
    for k in range(2):
        units = slice(k * HALF, (k + 1) * HALF)
        arrivals[4 + k].wait()
        arrivals[6 + k].wait()
        back = dot_nt(mine[:, high], w2_mine[units, :]) + dot_nt(send[:, high], w2_other[units, :])
        value = pre[:, units]
        square = value * value
        th = jnp.tanh(ROOT_TWO_PI * (value + CUBIC * square * value))
        half = 0.5 * (1.0 + th)
        slope = half + 0.5 * value * (1.0 - th * th) * ROOT_TWO_PI * (1.0 + 3.0 * CUBIC * square)
        d_pre = (back * slope).astype(BF)
        units_out[:, k * HALF:(k + 1) * HALF] = (value * half).astype(BF)
        units_out[:, (2 + k) * HALF:(3 + k) * HALF] = d_pre
        if k == 1:
            depart(mine, mine_out)
            depart(send, send_out.at[:, pl.ds(0, D)])
            depart(units_out, send_out.at[:, pl.ds(D, 2 * D)])
        terms = dot_nt(d_pre, w1_mine[:, units]), dot_nt(d_pre, w1_other[:, units])
        part_mine, part_other = terms if k == 0 else (part_mine + terms[0], part_other + terms[1])
    part_mine, part_other = part_mine.astype(BF), part_other.astype(BF)

    def finish(own, other):
        for columns, part in ((own, part_mine), (other, part_other)):
            if last:
                kept, away = parts

                @pl.when(flags_ref[1] == 0)
                def _():
                    kept[:, columns], away[:, columns] = part[:128], part[128:]

                @pl.when(flags_ref[1] != 0)
                def _():
                    kept[:, columns], away[:, columns] = part[128:], part[:128]
            else:
                parts[0][:, columns] = part

    both_orders(finish)
    for part, out in zip(parts, part_outs):
        depart(part, out)
    for copy in departures:
        copy.wait()


def expert_rows(last, flags, earlier, got, weights, cost=SMALL):
    rows = 256 if last else 192
    parts = [(128, D)] * 2 if last else [(192, D)]
    outs = [(rows, D), (rows, 3 * D), *parts]
    anywhere = pl.BlockSpec(memory_space=pl.ANY)
    buffers = [(HALF, D)] * 2 + [(D, HALF)] * 2 + [got.shape] + [(rows, D)] * 4 + [(rows, 2 * D)] + parts
    return pl.pallas_call(
        functools.partial(expert_kernel, last),
        in_specs=[
            pl.BlockSpec(memory_space=pltpu.SMEM), *[anywhere] * 6
        ],
        out_specs=(anywhere,) * len(outs),
        out_shape=tuple(hbm_shape(shape) for shape in outs),
        scratch_shapes=[
            *(pltpu.VMEM(shape, BF) for shape in buffers),
            pltpu.SemaphoreType.DMA((9,)),
            pltpu.SemaphoreType.DMA((5,)),
        ],
        compiler_params=params(40),
        cost_estimate=cost,
        name="expert_last" if last else "expert_main",
    )(flags, in_hbm(earlier), got, *(in_hbm(weight) for weight in weights))


def weight_grads_kernel(*refs):
    *operands, in_ref, out_ref = refs
    tokens, grads, hidden, d_pre = (
        jnp.concatenate([ref[...] for ref in operands[i::4]], axis=0) for i in range(4)
    )
    in_ref[...] = dot_tn(tokens, d_pre).astype(BF)
    out_ref[...] = dot_tn(hidden, grads).astype(BF)


def weight_grads(sets):
    specs, operands = [], []

    def take(x, block, moves):
        operands.append(in_hbm(x))
        index = (lambda h: (0, block + h)) if moves else (lambda h: (0, block))
        specs.append(pl.BlockSpec((x.shape[0], HALF), index))

    for mine, send, received in sets:
        for near, far in ((mine, send), (received, received)):
            take(near, 0, False)
            take(near, 1, False)
            take(far, 2, True)
            take(far, 4, True)
    return pl.pallas_call(
        weight_grads_kernel,
        grid=(2,),
        in_specs=specs,
        out_specs=(
            pl.BlockSpec((HALF, HALF), lambda h: (0, h)),
            pl.BlockSpec((HALF, HALF), lambda h: (h, 0)),
        ),
        out_shape=(hbm_shape((HALF, D)), hbm_shape((D, HALF))),
        compiler_params=params(48),
        cost_estimate=SMALL,
        name="weight_grads",
    )(*operands)


def merge_kernel(main_a, main_b, last_a, last_b, out_ref):
    row, column = iota((256, 128), 0), iota((256, 128), 1)
    target = ((column & 31) << 3) + (column >> 5)
    row6, column6 = iota((256, 192), 0), iota((256, 192), 1)
    spread = mask(row6 == ((column6 & 31) << 3) + (column6 >> 5))
    three = (main_a[...].astype(F32) + main_b[...].astype(F32)).astype(BF)
    two = (last_a[...].astype(F32) + last_b[...].astype(F32)).astype(BF)
    four = jnp.concatenate([three, two[:32]], axis=0)
    folded = dot(mask(row == target), four[:, :768]) + dot(mask(row == target + 4), four[:, 768:])
    out_ref[:, :768] = folded.astype(BF)
    fifth = jnp.concatenate([two[32:, j * 256:(j + 1) * 256] for j in range(6)], axis=0)
    out_ref[:, 768:] = dot(spread, fifth).astype(BF)


def merge(*parts):
    return pl.pallas_call(
        merge_kernel,
        grid=(2,),
        in_specs=[pl.BlockSpec((rows, D), lambda g: (g, 0)) for rows in (96, 96, 64, 64)],
        out_specs=pl.BlockSpec((256, 1024), lambda g: (g, 0)),
        out_shape=hbm_shape((512, 1024)),
        compiler_params=params(),
        cost_estimate=SMALL,
        name="merge",
    )(in_hbm(parts[0]), parts[1], in_hbm(parts[2]), parts[3])


def combine_kernel(routes_ref, got_ref, earlier_ref, out_ref):
    _, match, rank = slot_matches(routes_ref[...])
    inner = iota((EXPERTS * 8, TOK), 0) & 7
    chosen = match & (rank == (inner & 3).astype(F32))
    sides = [mask(chosen & (inner < 4)), mask(chosen & (inner >= 4))]
    chosen = match & (rank == 4.0)
    for j in range(6):
        columns = slice((j % 3) * 256, (j % 3 + 1) * 256)
        total = dot_tn(sides[j // 3], got_ref[:, columns])
        total += dot_tn(mask(chosen & (inner == j)), got_ref[:, 768:])
        out_ref[:, j * 256:(j + 1) * 256] = total.astype(BF)


def combine(routes_t, got, earlier):
    return pl.pallas_call(
        combine_kernel,
        in_specs=[whole(routes_t.shape), whole(got.shape), pl.BlockSpec(memory_space=pl.ANY)],
        out_specs=whole((TOK, D)),
        out_shape=jax.ShapeDtypeStruct((TOK, D), BF),
        compiler_params=params(),
        cost_estimate=SMALL,
        name="combine",
    )(routes_t, got, in_hbm(earlier))


def per_device(tokens, out_grad, routes, gate_probs, weight_in, weight_out):
    chips = [(i, i ^ 1) for i in range(128)]
    cores = [(0, 1), (1, 0)]
    outer = [4 * i + x for i in range(32) for x in (0, 3)]
    inner = [4 * i + x for i in range(32) for x in (1, 2)]
    halves, everyone = [outer, inner], [outer + inner]
    place = lax.axis_index("expert") & 3
    group = jnp.where((place == 1) | (place == 2), 1, 0)
    flags = jnp.stack([lax.axis_index("dp"), group]).astype(jnp.int32)

    def exchange(rows, groups):
        count = len(groups[0])
        chunked = rows.reshape(count, rows.shape[0] // count, rows.shape[1])
        got = lax.all_to_all(
            chunked, "expert", split_axis=0, concat_axis=0, tiled=True, axis_index_groups=groups
        )
        return got.reshape(rows.shape)

    def to_other_core(x):
        return lax.ppermute(x, "dp", cores)

    routes_t, gates_t = routes.T, gate_probs.T
    send_main = pack(False, routes_t, gates_t, tokens, out_grad)
    send_last = pack(True, routes_t, gates_t, tokens, out_grad)
    weight_sent = after(weight_out, send_last)
    weights = (weight_in, to_other_core(weight_in), weight_out, to_other_core(weight_sent))
    own_got = exchange(send_main, halves)
    pair_got = lax.ppermute(own_got, "expert", chips)
    own_mine, own_send, own_part = expert_rows(False, flags, send_main, own_got, weights)
    last_got = exchange(send_last, everyone)
    pair_mine, pair_send, pair_part = expert_rows(False, flags, own_part, pair_got, weights, LARGE)
    other_main = lax.ppermute(pair_part, "expert", chips)
    last_mine, last_send, last_part, last_away = expert_rows(True, flags, pair_part, last_got, weights)
    other_last = lax.ppermute(last_away, "expert", chips)
    merged = merge(own_part, other_main, last_part, other_last)
    got = exchange(merged, halves)
    grad_in, grad_out = weight_grads([
        (own_mine, own_send, to_other_core(own_send)),
        (pair_mine, pair_send, to_other_core(pair_send)),
        (after(last_mine, merged), last_send, to_other_core(last_send)),
    ])
    return combine(routes_t, got, grad_in), grad_in, grad_out


def solution(mesh):
    return jax.shard_map(
        per_device,
        mesh=mesh,
        in_specs=(
            P(("dp", "expert"), None),
            P(("dp", "expert"), None),
            P(("dp", "expert"), None),
            P(("dp", "expert"), None),
            P("dp", "expert"),
            P("expert", "dp"),
        ),
        out_specs=(P(("dp", "expert"), None), P("dp", "expert"), P("expert", "dp")),
        check_vma=False,
    )
```
